32 devices in a mesh: gx: 4 (over y, core), gy: 8 (over z, x).
Axes of the slice: x: 2, y: 2, z: 4, core: 2. Of those that a mesh axis runs over, the one named last changes fastest.
Arguments:
- site_tensors: bfloat16 [32, 16, 256, 256], P('gx', 'gy'), may hold values from -6 to 6
- test_matrix: bfloat16 [32, 16, 16, 256], P('gx', 'gy'), may hold values from -0.375 to 0.375
Outputs:
- coarse: bfloat16 [16, 16, 256, 256], P('gx', 'gy')
- log_norm: float32 [16, 16], P('gx', 'gy')
- trace: float32 [16, 16], P('gx', 'gy')
The draws below stay inside these ranges and needn't reach their ends.
All inputs are finite; a program needn't handle non-finite values.
Results may differ from the reference program's by a relative error of at most 0.0086.
Values may be sent and summed in bfloat16 or wider, within the bound.
A program may use at most 64 MiB of HBM per device.

```python
import jax
import jax.numpy as jnp
from jax import lax

CHI = 16
NX = 32
NY = 16


def level_of(key, shape, split, least, high):
    factor_of, own = 1.0, jax.random.fold_in(key, 6)
    for position, parts in split:
        steps = jnp.exp(jax.random.uniform(jax.random.fold_in(own, position), (parts,), jnp.float32, least / len(split), high / len(split)))
        factor_of = factor_of * jnp.repeat(steps, shape[position] // parts).reshape([-1 if axis == position else 1 for axis in range(len(shape))])
    return factor_of


def gaussian(own_key, dims, deviation, limit, pieces=(), kind=jnp.bfloat16):
    drawn = jax.random.normal(own_key, dims, jnp.float32) * deviation
    if len(pieces) > 0:
        drawn = level_of(own_key, dims, pieces, -0.22, 0.18) * drawn
    return jnp.clip(drawn, min=-limit, max=limit).astype(kind)


def setup_inputs(seed: int = 0) -> dict:
    arg_keys = jax.random.split(jax.random.key(seed), 3)
    site_tensors = gaussian(arg_keys[0], (NX, NY, CHI * CHI, CHI * CHI), 1.0, 6.0, ((0, 4), (1, 8)))
    test_matrix = gaussian(arg_keys[1], (NX, NY, CHI, CHI * CHI), (CHI * CHI) ** -0.5, 0.375, ((0, 4), (1, 8)))
    return dict(site_tensors=site_tensors, test_matrix=test_matrix)


def split_sites(tensors, tests):
    wide = tensors.astype(jnp.float32)
    sketch = jnp.einsum('sij,skj->sik', wide, tests.astype(jnp.float32), precision=lax.Precision.HIGHEST)
    gram_matrix = jnp.einsum('sik,sil->skl', sketch, sketch, precision=lax.Precision.HIGHEST)
    lower_factor = jnp.linalg.cholesky(gram_matrix)
    basis = jax.scipy.linalg.solve_triangular(lower_factor, jnp.swapaxes(sketch, 1, 2), lower=True).astype(jnp.bfloat16)
    second = jnp.einsum('ski,sij->skj', basis.astype(jnp.float32), wide, precision=lax.Precision.HIGHEST).astype(jnp.bfloat16)
    return jnp.stack([basis, second], axis=1)

def pick_sites(halves):
    rows = halves.shape[1]
    paired = halves.reshape(halves.shape[0] // 2, 2, rows, 2, CHI, CHI * CHI)
    odd_rows = (jnp.arange(rows) % 2 == 1)[None, :, None, None, None]
    return jnp.where(odd_rows, paired[:, 1], paired[:, 0])

def contract_sites(first, second, third, fourth):
    count = first.shape[0]
    north_east = first[:, 0].reshape(count, CHI, CHI, CHI).astype(jnp.float32)
    north_west = second[:, 0].reshape(count, CHI, CHI, CHI).astype(jnp.float32)
    south_east = third[:, 1].reshape(count, CHI, CHI, CHI).astype(jnp.float32)
    south_west = fourth[:, 1].reshape(count, CHI, CHI, CHI).astype(jnp.float32)
    pair_low = jnp.einsum('naur,nbvr->nabuv', north_east, north_west, precision=lax.Precision.HIGHEST).astype(jnp.bfloat16)
    pair_high = jnp.einsum('ncru,nevr->nceuv', south_east, south_west, precision=lax.Precision.HIGHEST).astype(jnp.bfloat16)
    pair_low = pair_low.reshape(count, CHI * CHI, CHI * CHI).astype(jnp.float32)
    pair_high = pair_high.reshape(count, CHI * CHI, CHI * CHI).astype(jnp.float32)
    raw = jnp.einsum('nij,nkj->nik', pair_low, pair_high, precision=lax.Precision.HIGHEST)
    squares = lax.optimization_barrier(jnp.sum(raw * raw, axis=(1, 2)))
    norm_value = jnp.sqrt(squares + 1e-06)
    identity = jnp.eye(CHI, dtype=jnp.float32)
    trace_mask = identity[:, None, None, :] * identity[None, :, :, None]
    traced = lax.optimization_barrier(jnp.sum(raw.reshape(count, CHI, CHI, CHI, CHI) * trace_mask[None], axis=(1, 2, 3, 4)))
    coarse = (CHI * CHI * raw / norm_value[:, None, None]).astype(jnp.bfloat16)
    return (coarse, jnp.log(norm_value), CHI * traced / norm_value)

def reference(site_tensors, test_matrix):

    def split_column(packed):
        column_tensors, column_tests = packed
        return split_sites(column_tensors, column_tests)
    halves = lax.map(split_column, (site_tensors, test_matrix))
    right_sites = jnp.roll(halves, -1, axis=0)
    upper_sites = jnp.roll(halves, -1, axis=1)
    corner_sites = jnp.roll(right_sites, -1, axis=1)
    picked = (pick_sites(halves), pick_sites(right_sites), pick_sites(upper_sites), pick_sites(corner_sites))

    def contract_column(packed):
        return contract_sites(packed[0], packed[1], packed[2], packed[3])
    coarse, log_norm, trace = lax.map(contract_column, picked)
    return (coarse, log_norm, trace)
```

```python
import jax
import jax.numpy as jnp
from jax import lax
from jax.experimental import pallas as pl
from jax.experimental.pallas import tpu as pltpu
from jax.sharding import PartitionSpec as P

CHI = 16
WIDE = CHI * CHI
HALF = WIDE // 2
MESH = pl.DeviceIdType.MESH
F32 = jnp.float32
BF16 = jnp.bfloat16
NT = (((1,), (1,)), ((), ()))
NN = (((1,), (0,)), ((), ()))


def iota(shape, axis):
    return lax.broadcasted_iota(jnp.int32, shape, axis)


def swap_chunks(rows):
    rows = list(rows)
    chunk = iota(rows[0].shape, 1) // CHI
    for step in (4, 2, 1):
        low = (chunk & step) == 0
        for i in range(8):
            if i & step:
                continue
            first, other = rows[i], rows[i + step]
            rows[i] = jnp.where(low, first, pltpu.roll(other, CHI * step, 1))
            rows[i + step] = jnp.where(low, pltpu.roll(first, HALF - CHI * step, 1), other)
    return rows


def spread(halves):
    parts = []
    for side in range(2):
        parts += swap_chunks([h[:, side * HALF:(side + 1) * HALF].astype(F32) for h in halves])
    return jnp.concatenate(parts, axis=0).astype(BF16)


def regroup(x):
    columns = []
    for upper in range(2):
        column = []
        for side in range(2):
            column += swap_chunks([
                x[(upper * 8 + v) * CHI:(upper * 8 + v + 1) * CHI, side * HALF:(side + 1) * HALF]
                for v in range(8)
            ])
        columns.append(jnp.concatenate(column, axis=0).astype(BF16))
    return jnp.concatenate(columns, axis=1)


def eliminate(gram):
    row = iota(gram.shape, 0)
    lane = iota(gram.shape, 1)
    inverse = jnp.where(row == lane % CHI, 1.0, 0.0).astype(F32)
    pivots = gram
    for k in range(CHI):
        column = jnp.take_along_axis(gram, lane // CHI * CHI + k, axis=1)
        pivot = column[k:k + 1, :]
        pivots = jnp.where(row == k, pivot, pivots)
        factor = jnp.where(row > k, column * (1.0 / pivot), 0.0)
        inverse = inverse - factor * inverse[k:k + 1, :]
        gram = gram - factor * gram[k:k + 1, :]
    return inverse * lax.rsqrt(pivots)


def kernel(
    nx, ny, tensors_ref, tests_ref, coarse_ref, log_ref, trace_ref,
    held, basis_ref, low_ref, up_ref, halo_basis, halo_second, pair_a, pair_b, stage,
    in_sem, out_sem, send_sem, recv_sem,
):
    mx, my = lax.axis_index("gx"), lax.axis_index("gy")
    right, left = lax.rem(mx + 1, nx), lax.rem(mx + nx - 1, nx)
    above, below = lax.rem(my + 1, ny), lax.rem(my + ny - 1, ny)
    loads = [
        pltpu.make_async_copy(tensors_ref.at[pl.ds(2 * c, 2)], held.at[pl.ds(2 * c, 2)], in_sem.at[c])
        for c in range(4)
    ]
    for load in loads:
        load.start()
    barrier = pltpu.get_barrier_semaphore()
    for target in ((right, my), (mx, above), (right, above)):
        pl.semaphore_signal(barrier, inc=1, device_id=target, device_id_type=MESH)

    sketches = []
    for x in range(8):
        if x % 2 == 0:
            loads[x // 2].wait()
        for y in range(2):
            sketches.append(lax.dot_general(tests_ref[x, y], held[x, y], NT, preferred_element_type=F32))
    sketch = jnp.concatenate(sketches, axis=0)
    inverses = []
    for side in range(2):
        part = sketch[side * HALF:(side + 1) * HALF]
        product = lax.dot_general(part, part, NT, precision=lax.Precision.HIGHEST, preferred_element_type=F32)
        chunk = iota((CHI, HALF), 1) // CHI
        gram = jnp.zeros((CHI, HALF), F32)
        for n in range(8):
            gram = gram + jnp.where(chunk == n, product[n * CHI:(n + 1) * CHI], 0.0)
        inverse = eliminate(gram)
        block = jnp.concatenate([jnp.where(chunk == n, inverse, 0.0) for n in range(8)], axis=0)
        basis = lax.dot_general(block, part, NN, precision=lax.Precision.HIGHEST, preferred_element_type=F32)
        basis_ref[pl.ds(8 * side, 8)] = basis.astype(BF16).reshape(8, CHI, WIDE)

    pl.semaphore_wait(barrier, 3)
    copies = [
        pltpu.make_async_remote_copy(
            basis_ref.at[1], halo_basis.at[0], send_sem.at[0], recv_sem.at[0],
            device_id=(left, my), device_id_type=MESH),
        pltpu.make_async_remote_copy(
            low_ref.at[0], halo_second.at[7], send_sem.at[1], recv_sem.at[1],
            device_id=(left, below), device_id_type=MESH),
        pltpu.make_async_remote_copy(
            low_ref.at[pl.ds(1, 7)], halo_second.at[pl.ds(0, 7)], send_sem.at[2], recv_sem.at[2],
            device_id=(mx, below), device_id_type=MESH),
    ]
    copies[0].start()
    for x in range(8):
        low_ref[x] = jnp.dot(basis_ref[2 * x], held[x, 0], preferred_element_type=F32).astype(BF16)
        if x == 0:
            copies[1].start()
    copies[2].start()
    for x in range(8):
        up_ref[x] = jnp.dot(basis_ref[2 * x + 1], held[x, 1], preferred_element_type=F32).astype(BF16)

    flip = (iota((WIDE, WIDE), 0) // CHI == iota((WIDE, WIDE), 1) % CHI) & (
        iota((WIDE, WIDE), 0) % CHI == iota((WIDE, WIDE), 1) // CHI)
    flip_wide = jnp.where(flip, 1.0, 0.0).astype(F32)
    flip_matrix = flip_wide.astype(BF16)
    at_row, at_col = iota((8, 128), 0), iota((8, 128), 1)

    def outgoing(p, g):
        return pltpu.make_async_copy(stage.at[p, g], coarse_ref.at[p, g], out_sem.at[p, g])

    def contract(g, north_east, north_west, south_east, south_west, sums):
        turned = jnp.dot(jnp.concatenate(south_east, axis=0), flip_matrix, preferred_element_type=F32)
        turned = [turned[q * CHI:(q + 1) * CHI] for q in range(4)]
        left_side = spread(north_east + turned)
        left_side = jnp.dot(flip_matrix, left_side, preferred_element_type=F32).astype(BF16)
        right_side = spread(north_west + south_west)
        pair_a[...] = left_side
        pair_b[...] = right_side

        def plaquette(p, sums):
            squares, traces = sums
            chunk = iota((WIDE, HALF), 1) // CHI
            pairs = []
            for q in (p, p + 4):
                masked = jnp.where(chunk == q, pair_b[...], jnp.zeros((), BF16))
                x = lax.dot_general(masked, pair_a[...], NT, preferred_element_type=F32)
                pairs.append(regroup(x))
            raw = lax.dot_general(pairs[0], pairs[1], NT, preferred_element_type=F32)
            square = jnp.sum(jnp.sum(raw * raw, axis=0, keepdims=True), axis=1, keepdims=True) + 1e-6
            traced = jnp.sum(jnp.sum(raw * flip_wide, axis=0, keepdims=True), axis=1, keepdims=True)
            stage[p, g] = (raw * (WIDE * lax.rsqrt(square))).astype(BF16)
            outgoing(p, g).start()
            here = (at_row == p) & (at_col == g)
            return jnp.where(here, square, squares), jnp.where(here, traced, traces)

        return lax.fori_loop(0, 4, plaquette, sums)

    sums = (jnp.ones((8, 128), F32), jnp.zeros((8, 128), F32))
    sums = contract(
        0,
        [basis_ref[4 * p] for p in range(4)],
        [basis_ref[4 * p + 2] for p in range(4)],
        [up_ref[2 * p] for p in range(4)],
        [up_ref[2 * p + 1] for p in range(4)],
        sums,
    )
    for copy in copies:
        copy.wait()
    sums = contract(
        1,
        [basis_ref[4 * p + 3] for p in range(4)],
        [basis_ref[4 * p + 5] for p in range(3)] + [halo_basis[0]],
        [halo_second[2 * p] for p in range(4)],
        [halo_second[2 * p + 1] for p in range(4)],
        sums,
    )
    norm = jnp.sqrt(sums[0])
    log_ref[...] = jnp.log(norm)[:4, :2]
    trace_ref[...] = (CHI * sums[1] / norm)[:4, :2]
    for g in range(2):
        for p in range(4):
            outgoing(p, g).wait()


def solution(mesh):
    nx, ny = mesh.shape["gx"], mesh.shape["gy"]

    def body(site_tensors, test_matrix):
        vmem = pl.BlockSpec(memory_space=pltpu.VMEM)
        anywhere = pl.BlockSpec(memory_space=pl.ANY)
        return pl.pallas_call(
            lambda *refs: kernel(nx, ny, *refs),
            out_shape=(
                jax.ShapeDtypeStruct((4, 2, WIDE, WIDE), BF16),
                jax.ShapeDtypeStruct((4, 2), F32),
                jax.ShapeDtypeStruct((4, 2), F32),
            ),
            in_specs=[anywhere, vmem],
            out_specs=(anywhere, vmem, vmem),
            scratch_shapes=[
                pltpu.VMEM((8, 2, WIDE, WIDE), BF16),
                pltpu.VMEM((16, CHI, WIDE), BF16),
                pltpu.VMEM((8, CHI, WIDE), BF16),
                pltpu.VMEM((8, CHI, WIDE), BF16),
                pltpu.VMEM((1, CHI, WIDE), BF16),
                pltpu.VMEM((8, CHI, WIDE), BF16),
                pltpu.VMEM((WIDE, HALF), BF16),
                pltpu.VMEM((WIDE, HALF), BF16),
                pltpu.VMEM((4, 2, WIDE, WIDE), BF16),
                pltpu.SemaphoreType.DMA((4,)),
                pltpu.SemaphoreType.DMA((4, 2)),
                pltpu.SemaphoreType.DMA((3,)),
                pltpu.SemaphoreType.DMA((3,)),
            ],
            compiler_params=pltpu.CompilerParams(
                collective_id=0, has_side_effects=True, vmem_limit_bytes=32 * 2**20),
            cost_estimate=pl.CostEstimate(
                flops=1_000_000_000, bytes_accessed=4_000_000, transcendentals=0),
        )(site_tensors, test_matrix)

    in_specs = (P("gx", "gy", None, None), P("gx", "gy", None, None))
    out_specs = (P("gx", "gy", None, None), P("gx", "gy"), P("gx", "gy"))
    return jax.shard_map(body, mesh=mesh, in_specs=in_specs, out_specs=out_specs, check_vma=False)
```

```python
import jax
import jax.numpy as jnp
from jax import lax
from jax.experimental import pallas as pl
from jax.experimental.pallas import tpu as pltpu
from jax.sharding import PartitionSpec as P

CHI = 16
WIDE = CHI * CHI
HALF = WIDE // 2
MESH = pl.DeviceIdType.MESH
F32 = jnp.float32
BF16 = jnp.bfloat16
NT = (((1,), (1,)), ((), ()))
NN = (((1,), (0,)), ((), ()))


def iota(shape, axis):
    return lax.broadcasted_iota(jnp.int32, shape, axis)


def swap_chunks(rows):
    rows = list(rows)
    chunk = iota(rows[0].shape, 1) // CHI
    for step in (4, 2, 1):
        low = (chunk & step) == 0
        for i in range(8):
            if i & step:
                continue
            first, other = rows[i], rows[i + step]
            rows[i] = jnp.where(low, first, pltpu.roll(other, CHI * step, 1))
            rows[i + step] = jnp.where(low, pltpu.roll(first, HALF - CHI * step, 1), other)
    return rows


def spread(halves):
    parts = []
    for side in range(2):
        parts += swap_chunks([h[:, side * HALF:(side + 1) * HALF] for h in halves])
    return jnp.concatenate(parts, axis=0)


def regroup(x):
    columns = []
    for upper in range(2):
        column = []
        for side in range(2):
            column += swap_chunks([
                x[(upper * 8 + v) * CHI:(upper * 8 + v + 1) * CHI, side * HALF:(side + 1) * HALF]
                for v in range(8)
            ])
        columns.append(jnp.concatenate(column, axis=0))
    return jnp.concatenate(columns, axis=1)


def eliminate(grams):
    row = iota(grams[0].shape, 0)
    lane = iota(grams[0].shape, 1)
    grams = list(grams)
    inverses = [jnp.where(row == lane % CHI, 1.0, 0.0).astype(F32)] * len(grams)
    pivots = list(grams)
    for k in range(CHI):
        for s in range(len(grams)):
            column = jnp.take_along_axis(grams[s], lane // CHI * CHI + k, axis=1)
            pivot = column[k:k + 1, :]
            pivots[s] = jnp.where(row == k, pivot, pivots[s])
            factor = jnp.where(row > k, column * (1.0 / pivot), 0.0)
            inverses[s] = inverses[s] - factor * inverses[s][k:k + 1, :]
            grams[s] = grams[s] - factor * grams[s][k:k + 1, :]
    return [i * lax.rsqrt(p) for i, p in zip(inverses, pivots)]


def kernel(
    nx, ny, tensors_ref, tests_ref, coarse_ref, log_ref, trace_ref,
    held, basis_ref, low_ref, up_ref, halo_basis, halo_second, pair_a, pair_b, stage,
    tests, in_sem, out_sem, send_sem, recv_sem,
):
    mx, my = lax.axis_index("gx"), lax.axis_index("gy")
    right, left = lax.rem(mx + 1, nx), lax.rem(mx + nx - 1, nx)
    above, below = lax.rem(my + 1, ny), lax.rem(my + ny - 1, ny)
    loads = [pltpu.make_async_copy(tensors_ref.at[c], held.at[c], in_sem.at[c]) for c in range(8)]
    loads.append(pltpu.make_async_copy(tests_ref, tests, in_sem.at[8]))
    loads[8].start()
    for load in loads[:8]:
        load.start()
    barrier = pltpu.get_barrier_semaphore()
    for target in ((right, my), (mx, above), (right, above)):
        pl.semaphore_signal(barrier, inc=1, device_id=target, device_id_type=MESH)

    sketches = []
    loads[8].wait()
    for x in range(8):
        loads[x].wait()
        for y in range(2):
            sketches.append(lax.dot_general(tests[x, y], held[x, y], NT, preferred_element_type=F32))
    sketch = jnp.concatenate(sketches, axis=0)
    chunk = iota((CHI, HALF), 1) // CHI
    grams = []
    for side in range(2):
        part = sketch[side * HALF:(side + 1) * HALF]
        product = lax.dot_general(part, part, NT, precision=lax.Precision.HIGHEST, preferred_element_type=F32)
        gram = jnp.zeros((CHI, HALF), F32)
        for n in range(8):
            gram = gram + jnp.where(chunk == n, product[n * CHI:(n + 1) * CHI], 0.0)
        grams.append(gram)
    for side, inverse in enumerate(eliminate(grams)):
        part = sketch[side * HALF:(side + 1) * HALF]
        block = jnp.concatenate([jnp.where(chunk == n, inverse, 0.0) for n in range(8)], axis=0)
        basis = lax.dot_general(block, part, NN, precision=lax.Precision.HIGHEST, preferred_element_type=F32)
        basis_ref[pl.ds(8 * side, 8)] = basis.astype(BF16).reshape(8, CHI, WIDE)

    pl.semaphore_wait(barrier, 3)
    copies = [
        pltpu.make_async_remote_copy(
            basis_ref.at[1], halo_basis.at[0], send_sem.at[0], recv_sem.at[0],
            device_id=(left, my), device_id_type=MESH),
        pltpu.make_async_remote_copy(
            low_ref.at[0], halo_second.at[7], send_sem.at[1], recv_sem.at[1],
            device_id=(left, below), device_id_type=MESH),
        pltpu.make_async_remote_copy(
            low_ref.at[pl.ds(1, 7)], halo_second.at[pl.ds(0, 7)], send_sem.at[2], recv_sem.at[2],
            device_id=(mx, below), device_id_type=MESH),
    ]
    copies[0].start()
    for x in range(8):
        low_ref[x] = jnp.dot(basis_ref[2 * x], held[x, 0], preferred_element_type=F32).astype(BF16)
        if x == 0:
            copies[1].start()
    copies[2].start()
    for x in range(8):
        up_ref[x] = jnp.dot(basis_ref[2 * x + 1], held[x, 1], preferred_element_type=F32).astype(BF16)

    flip = (iota((WIDE, WIDE), 0) // CHI == iota((WIDE, WIDE), 1) % CHI) & (
        iota((WIDE, WIDE), 0) % CHI == iota((WIDE, WIDE), 1) // CHI)
    flip_wide = jnp.where(flip, 1.0, 0.0).astype(F32)
    flip_matrix = flip_wide.astype(BF16)
    at_row, at_col = iota((8, 128), 0), iota((8, 128), 1)

    def outgoing(p, g):
        return pltpu.make_async_copy(stage.at[p, g], coarse_ref.at[p, g], out_sem.at[p, g])

    def contract(g, north_east, north_west, south_east, south_west, sums):
        turned = jnp.dot(jnp.concatenate(south_east, axis=0), flip_matrix, preferred_element_type=F32).astype(BF16)
        turned = [turned[q * CHI:(q + 1) * CHI] for q in range(4)]
        left_side = spread(north_east + turned)
        left_side = jnp.dot(flip_matrix, left_side, preferred_element_type=F32).astype(BF16)
        right_side = spread(north_west + south_west)
        pair_a[...] = left_side
        pair_b[...] = right_side

        chunk = iota((WIDE, HALF), 1) // CHI

        def paired(p):
            pairs = []
            for q in (p, p + 4):
                masked = jnp.where(chunk == q, pair_b[...], jnp.zeros((), BF16))
                x = lax.dot_general(masked, pair_a[...], NT, preferred_element_type=F32)
                pairs.append(regroup(x.astype(BF16)))
            return pairs

        def finish(p, pairs, sums):
            squares, traces = sums
            raw = lax.dot_general(pairs[0], pairs[1], NT, preferred_element_type=F32)
            square = jnp.sum(jnp.sum(raw * raw, axis=0, keepdims=True), axis=1, keepdims=True) + 1e-6
            traced = jnp.sum(jnp.sum(raw * flip_wide, axis=0, keepdims=True), axis=1, keepdims=True)
            stage[p, g] = (raw * (WIDE * lax.rsqrt(square))).astype(BF16)
            outgoing(p, g).start()
            here = (at_row == p) & (at_col == g)
            return jnp.where(here, square, squares), jnp.where(here, traced, traces)

        ahead = paired(0)
        for p in range(4):
            pairs, ahead = ahead, paired(p + 1) if p < 3 else None
            sums = finish(p, pairs, sums)
        return sums

    sums = (jnp.ones((8, 128), F32), jnp.zeros((8, 128), F32))
    sums = contract(
        0,
        [basis_ref[4 * p] for p in range(4)],
        [basis_ref[4 * p + 2] for p in range(4)],
        [up_ref[2 * p] for p in range(4)],
        [up_ref[2 * p + 1] for p in range(4)],
        sums,
    )
    for copy in copies:
        copy.wait()
    sums = contract(
        1,
        [basis_ref[4 * p + 3] for p in range(4)],
        [basis_ref[4 * p + 5] for p in range(3)] + [halo_basis[0]],
        [halo_second[2 * p] for p in range(4)],
        [halo_second[2 * p + 1] for p in range(4)],
        sums,
    )
    norm = jnp.sqrt(sums[0])
    log_ref[...] = jnp.log(norm)[:4, :2]
    trace_ref[...] = (CHI * sums[1] / norm)[:4, :2]
    for g in range(2):
        for p in range(4):
            outgoing(p, g).wait()


def solution(mesh):
    nx, ny = mesh.shape["gx"], mesh.shape["gy"]

    def body(site_tensors, test_matrix):
        vmem = pl.BlockSpec(memory_space=pltpu.VMEM)
        hbm = pl.BlockSpec(memory_space=pltpu.HBM)
        return pl.pallas_call(
            lambda *refs: kernel(nx, ny, *refs),
            out_shape=(
                jax.ShapeDtypeStruct((4, 2, WIDE, WIDE), BF16),
                jax.ShapeDtypeStruct((4, 2), F32),
                jax.ShapeDtypeStruct((4, 2), F32),
            ),
            in_specs=[hbm, hbm],
            out_specs=(hbm, vmem, vmem),
            scratch_shapes=[
                pltpu.VMEM((8, 2, WIDE, WIDE), BF16),
                pltpu.VMEM((16, CHI, WIDE), BF16),
                pltpu.VMEM((8, CHI, WIDE), BF16),
                pltpu.VMEM((8, CHI, WIDE), BF16),
                pltpu.VMEM((1, CHI, WIDE), BF16),
                pltpu.VMEM((8, CHI, WIDE), BF16),
                pltpu.VMEM((WIDE, HALF), BF16),
                pltpu.VMEM((WIDE, HALF), BF16),
                pltpu.VMEM((4, 2, WIDE, WIDE), BF16),
                pltpu.VMEM((8, 2, CHI, WIDE), BF16),
                pltpu.SemaphoreType.DMA((9,)),
                pltpu.SemaphoreType.DMA((4, 2)),
                pltpu.SemaphoreType.DMA((3,)),
                pltpu.SemaphoreType.DMA((3,)),
            ],
            compiler_params=pltpu.CompilerParams(
                collective_id=0, has_side_effects=True, vmem_limit_bytes=63 * 2**20),
            cost_estimate=pl.CostEstimate(
                flops=1_000_000_000, bytes_accessed=4_000_000, transcendentals=0),
        )(site_tensors, test_matrix)

    in_specs = (P("gx", "gy", None, None), P("gx", "gy", None, None))
    out_specs = (P("gx", "gy", None, None), P("gx", "gy"), P("gx", "gy"))
    return jax.shard_map(body, mesh=mesh, in_specs=in_specs, out_specs=out_specs, check_vma=False)
```

```python
import jax
import jax.numpy as jnp
from jax import lax
from jax.experimental import pallas as pl
from jax.experimental.pallas import tpu as pltpu
from jax.sharding import PartitionSpec as P

CHI = 16
WIDE = CHI * CHI
HALF = WIDE // 2
MESH = pl.DeviceIdType.MESH
F32 = jnp.float32
BF16 = jnp.bfloat16
NT = (((1,), (1,)), ((), ()))
NN = (((1,), (0,)), ((), ()))


def iota(shape, axis):
    return lax.broadcasted_iota(jnp.int32, shape, axis)


def swap_chunks(rows):
    rows = list(rows)
    chunk = iota(rows[0].shape, 1) // CHI
    for step in (4, 2, 1):
        low = (chunk & step) == 0
        for i in range(8):
            if i & step:
                continue
            first, other = rows[i], rows[i + step]
            rows[i] = jnp.where(low, first, pltpu.roll(other, CHI * step, 1))
            rows[i + step] = jnp.where(low, pltpu.roll(first, HALF - CHI * step, 1), other)
    return rows


def spread(halves):
    parts = []
    for side in range(2):
        parts += swap_chunks([h[:, side * HALF:(side + 1) * HALF] for h in halves])
    return jnp.concatenate(parts, axis=0)


def regroup(x):
    columns = []
    for upper in range(2):
        column = []
        for side in range(2):
            column += swap_chunks([
                x[(upper * 8 + v) * CHI:(upper * 8 + v + 1) * CHI, side * HALF:(side + 1) * HALF]
                for v in range(8)
            ])
        columns.append(jnp.concatenate(column, axis=0))
    return jnp.concatenate(columns, axis=1)


def eliminate(grams):
    row = iota(grams[0].shape, 0)
    lane = iota(grams[0].shape, 1)
    grams = list(grams)
    inverses = [jnp.where(row == lane % CHI, 1.0, 0.0).astype(F32)] * len(grams)
    pivots = list(grams)
    for k in range(CHI):
        for s in range(len(grams)):
            column = jnp.take_along_axis(grams[s], lane // CHI * CHI + k, axis=1)
            pivot = column[k:k + 1, :]
            pivots[s] = jnp.where(row == k, pivot, pivots[s])
            factor = jnp.where(row > k, column * (1.0 / pivot), 0.0)
            inverses[s] = inverses[s] - factor * inverses[s][k:k + 1, :]
            grams[s] = grams[s] - factor * grams[s][k:k + 1, :]
    return [i * lax.rsqrt(p) for i, p in zip(inverses, pivots)]


def flip_mask():
    row, col = iota((WIDE, WIDE), 0), iota((WIDE, WIDE), 1)
    return jnp.where((row // CHI == col % CHI) & (row % CHI == col // CHI), 1.0, 0.0).astype(F32)


def contract(g, north_east, north_west, south_east, south_west, sums, store):
    flip_wide = flip_mask()
    flip_matrix = flip_wide.astype(BF16)
    at_row, at_col = iota((8, 128), 0), iota((8, 128), 1)
    chunk = iota((WIDE, HALF), 1) // CHI
    turned = jnp.dot(jnp.concatenate(south_east, axis=0), flip_matrix, preferred_element_type=F32).astype(BF16)
    turned = [turned[q * CHI:(q + 1) * CHI] for q in range(4)]
    left_side = spread(north_east + turned)
    left_side = jnp.dot(flip_matrix, left_side, preferred_element_type=F32).astype(BF16)
    right_side = spread(north_west + south_west)
    left_turned, right_turned = left_side.T, right_side.T
    zero = jnp.zeros((), BF16)

    def paired(p):
        low = jnp.dot(jnp.where(chunk == p, right_side, zero), left_turned, preferred_element_type=F32)
        high = jnp.dot(jnp.where(chunk == p + 4, left_side, zero), right_turned, preferred_element_type=F32)
        return regroup(low.astype(BF16)), regroup(high.astype(BF16))

    def finish(p, pairs, sums):
        squares, traces = sums
        raw = jnp.dot(pairs[0], pairs[1], preferred_element_type=F32)
        square = jnp.sum(jnp.sum(raw * raw, axis=0, keepdims=True), axis=1, keepdims=True) + 1e-6
        traced = jnp.sum(jnp.sum(raw * flip_wide, axis=0, keepdims=True), axis=1, keepdims=True)
        store(p, (raw * (WIDE * lax.rsqrt(square))).astype(BF16))
        here = (at_row == g) & (at_col == p)
        return jnp.where(here, square, squares), jnp.where(here, traced, traces)

    ahead = paired(0)
    for p in range(4):
        pairs, ahead = ahead, paired(p + 1) if p < 3 else None
        sums = finish(p, pairs, sums)
    return sums


def split_kernel(
    nx, ny, tensors_ref, tests_ref, coarse_ref, sums_ref, ne_ref, nw_ref, halo_ref,
    held, basis_ref, low_ref, up_ref, halo_basis, halo_second, tests, in_sem, send_sem, recv_sem,
):
    mx, my = lax.axis_index("gx"), lax.axis_index("gy")
    right, left = lax.rem(mx + 1, nx), lax.rem(mx + nx - 1, nx)
    above, below = lax.rem(my + 1, ny), lax.rem(my + ny - 1, ny)
    loads = [pltpu.make_async_copy(tensors_ref.at[c], held.at[c], in_sem.at[c]) for c in range(8)]
    loads.append(pltpu.make_async_copy(tests_ref, tests, in_sem.at[8]))
    loads[8].start()
    for load in loads[:8]:
        load.start()
    barrier = pltpu.get_barrier_semaphore()
    for target in ((right, my), (mx, above), (right, above)):
        pl.semaphore_signal(barrier, inc=1, device_id=target, device_id_type=MESH)

    sketches = []
    loads[8].wait()
    for x in range(8):
        loads[x].wait()
        for y in range(2):
            sketches.append(lax.dot_general(tests[x, y], held[x, y], NT, preferred_element_type=F32))
    sketch = jnp.concatenate(sketches, axis=0)
    chunk = iota((CHI, HALF), 1) // CHI
    grams = []
    for side in range(2):
        part = sketch[side * HALF:(side + 1) * HALF]
        product = lax.dot_general(part, part, NT, precision=lax.Precision.HIGHEST, preferred_element_type=F32)
        gram = jnp.zeros((CHI, HALF), F32)
        for n in range(8):
            gram = gram + jnp.where(chunk == n, product[n * CHI:(n + 1) * CHI], 0.0)
        grams.append(gram)
    for side, inverse in enumerate(eliminate(grams)):
        part = sketch[side * HALF:(side + 1) * HALF]
        block = jnp.concatenate([jnp.where(chunk == n, inverse, 0.0) for n in range(8)], axis=0)
        basis = lax.dot_general(block, part, NN, precision=lax.Precision.HIGHEST, preferred_element_type=F32)
        basis_ref[pl.ds(8 * side, 8)] = basis.astype(BF16).reshape(8, CHI, WIDE)

    pl.semaphore_wait(barrier, 3)
    copies = [
        pltpu.make_async_remote_copy(
            basis_ref.at[1], halo_basis.at[0], send_sem.at[0], recv_sem.at[0],
            device_id=(left, my), device_id_type=MESH),
        pltpu.make_async_remote_copy(
            low_ref.at[0], halo_second.at[7], send_sem.at[1], recv_sem.at[1],
            device_id=(left, below), device_id_type=MESH),
        pltpu.make_async_remote_copy(
            low_ref.at[pl.ds(1, 7)], halo_second.at[pl.ds(0, 7)], send_sem.at[2], recv_sem.at[2],
            device_id=(mx, below), device_id_type=MESH),
    ]
    copies[0].start()
    for x in range(8):
        low_ref[x] = jnp.dot(basis_ref[2 * x], held[x, 0], preferred_element_type=F32).astype(BF16)
        if x == 0:
            copies[1].start()
    copies[2].start()
    for x in range(8):
        up_ref[x] = jnp.dot(basis_ref[2 * x + 1], held[x, 1], preferred_element_type=F32).astype(BF16)

    def store(p, value):
        coarse_ref[p] = value

    sums = (jnp.ones((8, 128), F32), jnp.zeros((8, 128), F32))
    sums = contract(
        0,
        [basis_ref[4 * p] for p in range(4)],
        [basis_ref[4 * p + 2] for p in range(4)],
        [up_ref[2 * p] for p in range(4)],
        [up_ref[2 * p + 1] for p in range(4)],
        sums,
        store,
    )
    sums_ref[0] = sums[0]
    sums_ref[1] = sums[1]
    for p in range(4):
        ne_ref[p] = basis_ref[4 * p + 3]
        if p < 3:
            nw_ref[p] = basis_ref[4 * p + 5]
    for copy in copies:
        copy.wait()
    nw_ref[3] = halo_basis[0]
    halo_ref[...] = halo_second[...]


def join_kernel(first_ref, sums_ref, ne_ref, nw_ref, halo_ref, coarse_ref, log_ref, trace_ref, stage, out_sem):
    early = [pltpu.make_async_copy(first_ref.at[p], coarse_ref.at[p, 0], out_sem.at[p]) for p in range(4)]
    late = [pltpu.make_async_copy(stage.at[p], coarse_ref.at[p, 1], out_sem.at[4 + p]) for p in range(4)]
    for copy in early:
        copy.start()

    def store(p, value):
        stage[p] = value
        late[p].start()

    squares, traces = contract(
        1,
        [ne_ref[p] for p in range(4)],
        [nw_ref[p] for p in range(4)],
        [halo_ref[2 * p] for p in range(4)],
        [halo_ref[2 * p + 1] for p in range(4)],
        (sums_ref[0], sums_ref[1]),
        store,
    )
    norm = jnp.sqrt(squares)
    log_ref[...] = jnp.log(norm)[:2, :4]
    trace_ref[...] = (CHI * traces / norm)[:2, :4]
    for copy in early + late:
        copy.wait()


def solution(mesh):
    nx, ny = mesh.shape["gx"], mesh.shape["gy"]
    vmem = pl.BlockSpec(memory_space=pltpu.VMEM)
    hbm = pl.BlockSpec(memory_space=pltpu.HBM)

    def body(site_tensors, test_matrix):
        site_tensors = pltpu.with_memory_space_constraint(site_tensors, pltpu.HBM)
        test_matrix = pltpu.with_memory_space_constraint(test_matrix, pltpu.HBM)
        between = pl.pallas_call(
            lambda *refs: split_kernel(nx, ny, *refs),
            out_shape=(
                pltpu.VMEM((4, WIDE, WIDE), BF16),
                pltpu.VMEM((2, 8, 128), F32),
                pltpu.VMEM((4, CHI, WIDE), BF16),
                pltpu.VMEM((4, CHI, WIDE), BF16),
                pltpu.VMEM((8, CHI, WIDE), BF16),
            ),
            in_specs=[hbm, hbm],
            out_specs=(vmem,) * 5,
            scratch_shapes=[
                pltpu.VMEM((8, 2, WIDE, WIDE), BF16),
                pltpu.VMEM((16, CHI, WIDE), BF16),
                pltpu.VMEM((8, CHI, WIDE), BF16),
                pltpu.VMEM((8, CHI, WIDE), BF16),
                pltpu.VMEM((1, CHI, WIDE), BF16),
                pltpu.VMEM((8, CHI, WIDE), BF16),
                pltpu.VMEM((8, 2, CHI, WIDE), BF16),
                pltpu.SemaphoreType.DMA((9,)),
                pltpu.SemaphoreType.DMA((3,)),
                pltpu.SemaphoreType.DMA((3,)),
            ],
            compiler_params=pltpu.CompilerParams(
                collective_id=0, has_side_effects=True, vmem_limit_bytes=24 * 2**20),
            cost_estimate=pl.CostEstimate(
                flops=700_000_000, bytes_accessed=3_000_000, transcendentals=0),
        )(site_tensors, test_matrix)
        between = [pltpu.with_memory_space_constraint(x, pltpu.VMEM) for x in between]
        coarse, log_norm, trace = pl.pallas_call(
            join_kernel,
            out_shape=(
                pltpu.HBM((4, 2, WIDE, WIDE), BF16),
                jax.ShapeDtypeStruct((2, 4), F32),
                jax.ShapeDtypeStruct((2, 4), F32),
            ),
            in_specs=[vmem] * 5,
            out_specs=(hbm, vmem, vmem),
            scratch_shapes=[
                pltpu.VMEM((4, WIDE, WIDE), BF16),
                pltpu.SemaphoreType.DMA((8,)),
            ],
            compiler_params=pltpu.CompilerParams(vmem_limit_bytes=24 * 2**20),
            cost_estimate=pl.CostEstimate(
                flops=300_000_000, bytes_accessed=1_000_000, transcendentals=0),
        )(*between)
        return coarse, log_norm.T, trace.T

    in_specs = (P("gx", "gy", None, None), P("gx", "gy", None, None))
    out_specs = (P("gx", "gy", None, None), P("gx", "gy"), P("gx", "gy"))
    return jax.shard_map(body, mesh=mesh, in_specs=in_specs, out_specs=out_specs, check_vma=False)
```

```python
import jax
import jax.numpy as jnp
from jax import lax
from jax.experimental import pallas as pl
from jax.experimental.pallas import tpu as pltpu
from jax.sharding import PartitionSpec as P

CHI = 16
WIDE = CHI * CHI
HALF = WIDE // 2
MESH = pl.DeviceIdType.MESH
F32 = jnp.float32
BF16 = jnp.bfloat16
NT = (((1,), (1,)), ((), ()))
NN = (((1,), (0,)), ((), ()))


def iota(shape, axis):
    return lax.broadcasted_iota(jnp.int32, shape, axis)


def swap_chunks(rows):
    rows = list(rows)
    chunk = iota(rows[0].shape, 1) // CHI
    for step in (4, 2, 1):
        low = (chunk & step) == 0
        for i in range(8):
            if i & step:
                continue
            first, other = rows[i], rows[i + step]
            rows[i] = jnp.where(low, first, pltpu.roll(other, CHI * step, 1))
            rows[i + step] = jnp.where(low, pltpu.roll(first, HALF - CHI * step, 1), other)
    return rows


def spread(halves):
    parts = []
    for side in range(2):
        parts += swap_chunks([h[:, side * HALF:(side + 1) * HALF] for h in halves])
    return jnp.concatenate(parts, axis=0)


def regroup(x):
    columns = []
    for upper in range(2):
        column = []
        for side in range(2):
            column += swap_chunks([
                x[(upper * 8 + v) * CHI:(upper * 8 + v + 1) * CHI, side * HALF:(side + 1) * HALF]
                for v in range(8)
            ])
        columns.append(jnp.concatenate(column, axis=0))
    return jnp.concatenate(columns, axis=1)


def eliminate(grams):
    row = iota(grams[0].shape, 0)
    lane = iota(grams[0].shape, 1)
    grams = list(grams)
    inverses = [jnp.where(row == lane % CHI, 1.0, 0.0).astype(F32)] * len(grams)
    pivots = list(grams)
    for k in range(0, CHI, 2):
        for s in range(len(grams)):
            gram, inverse = grams[s], inverses[s]
            first = jnp.take_along_axis(gram, lane // CHI * CHI + k, axis=1)
            second = jnp.take_along_axis(gram, lane // CHI * CHI + k + 1, axis=1)
            over = 1.0 / first[k:k + 1]
            first_factor = first * over
            shared = second[k:k + 1]
            second = second - first_factor * shared
            step = first_factor[k + 1:k + 2]
            gram_row, inverse_row = gram[k:k + 1], inverse[k:k + 1]
            gram_next = gram[k + 1:k + 2] - step * gram_row
            inverse_next = inverse[k + 1:k + 2] - step * inverse_row
            pivots[s] = jnp.where(row == k, first[k:k + 1], jnp.where(row == k + 1, second[k + 1:k + 2], pivots[s]))
            first_factor = jnp.where(row > k, first_factor, 0.0)
            second_factor = jnp.where(row > k + 1, second * (1.0 / second[k + 1:k + 2]), 0.0)
            grams[s] = gram - first_factor * gram_row - second_factor * gram_next
            inverses[s] = inverse - first_factor * inverse_row - second_factor * inverse_next
    return [i * lax.rsqrt(p) for i, p in zip(inverses, pivots)]


def flip_mask():
    row, col = iota((WIDE, WIDE), 0), iota((WIDE, WIDE), 1)
    return jnp.where((row // CHI == col % CHI) & (row % CHI == col // CHI), 1.0, 0.0).astype(F32)


def pair_sides(left, right):
    left = jnp.dot(flip_mask().astype(BF16), left, preferred_element_type=F32).astype(BF16)
    return left, right, left.T, right.T


def low_pair(sides, q):
    chunk = iota((WIDE, HALF), 1) // CHI
    masked = jnp.where(chunk == q, sides[1], jnp.zeros((), BF16))
    return regroup(jnp.dot(masked, sides[2], preferred_element_type=F32).astype(BF16))


def high_pair(sides, q):
    chunk = iota((WIDE, HALF), 1) // CHI
    masked = jnp.where(chunk == q, sides[0], jnp.zeros((), BF16))
    return regroup(jnp.dot(masked, sides[3], preferred_element_type=F32).astype(BF16))


def high_sides(south_east, south_west):
    turned = jnp.dot(
        jnp.concatenate(south_east, axis=0), flip_mask().astype(BF16), preferred_element_type=F32).astype(BF16)
    both = spread([turned[q * CHI:(q + 1) * CHI] for q in range(4)] + south_west)
    return pair_sides(both, pltpu.roll(both, HALF // 2, 1))


def finish(g, p, low, high, sums, store):
    squares, traces = sums
    raw = jnp.dot(low, high, preferred_element_type=F32)
    square = jnp.sum(jnp.sum(raw * raw, axis=0, keepdims=True), axis=1, keepdims=True) + 1e-6
    traced = jnp.sum(jnp.sum(raw * flip_mask(), axis=0, keepdims=True), axis=1, keepdims=True)
    store(p, (raw * (WIDE * lax.rsqrt(square))).astype(BF16))
    here = (iota((8, 128), 0) == g) & (iota((8, 128), 1) == p)
    return jnp.where(here, square, squares), jnp.where(here, traced, traces)


def split_kernel(
    nx, ny, tensors_ref, tests_ref, coarse_ref, sums_ref, lows_ref, last_ref, halo_ref,
    held, basis_ref, low_ref, up_ref, halo_basis, halo_second, tests, in_sem, send_sem, recv_sem,
):
    mx, my = lax.axis_index("gx"), lax.axis_index("gy")
    right, left = lax.rem(mx + 1, nx), lax.rem(mx + nx - 1, nx)
    above, below = lax.rem(my + 1, ny), lax.rem(my + ny - 1, ny)
    loads = [pltpu.make_async_copy(tensors_ref.at[c], held.at[c], in_sem.at[c]) for c in range(8)]
    loads.append(pltpu.make_async_copy(tests_ref, tests, in_sem.at[8]))
    loads[8].start()
    for load in loads[:8]:
        load.start()
    barrier = pltpu.get_barrier_semaphore()
    for target in ((right, my), (mx, above), (right, above)):
        pl.semaphore_signal(barrier, inc=1, device_id=target, device_id_type=MESH)

    sketches = []
    loads[8].wait()
    for x in range(8):
        loads[x].wait()
        for y in range(2):
            sketches.append(lax.dot_general(tests[x, y], held[x, y], NT, preferred_element_type=F32))
    sketch = jnp.concatenate(sketches, axis=0)
    chunk = iota((CHI, HALF), 1) // CHI
    grams = []
    for side in range(2):
        part = sketch[side * HALF:(side + 1) * HALF]
        product = lax.dot_general(part, part, NT, precision=lax.Precision.HIGHEST, preferred_element_type=F32)
        gram = jnp.zeros((CHI, HALF), F32)
        for n in range(8):
            gram = gram + jnp.where(chunk == n, product[n * CHI:(n + 1) * CHI], 0.0)
        grams.append(gram)
    for side, inverse in enumerate(eliminate(grams)):
        part = sketch[side * HALF:(side + 1) * HALF]
        block = jnp.concatenate([jnp.where(chunk == n, inverse, 0.0) for n in range(8)], axis=0)
        basis = lax.dot_general(block, part, NN, precision=lax.Precision.HIGHEST, preferred_element_type=F32)
        basis_ref[pl.ds(8 * side, 8)] = basis.astype(BF16).reshape(8, CHI, WIDE)

    pl.semaphore_wait(barrier, 3)
    copies = [
        pltpu.make_async_remote_copy(
            basis_ref.at[1], halo_basis.at[0], send_sem.at[0], recv_sem.at[0],
            device_id=(left, my), device_id_type=MESH),
        pltpu.make_async_remote_copy(
            low_ref.at[0], halo_second.at[7], send_sem.at[1], recv_sem.at[1],
            device_id=(left, below), device_id_type=MESH),
        pltpu.make_async_remote_copy(
            low_ref.at[pl.ds(1, 7)], halo_second.at[pl.ds(0, 7)], send_sem.at[2], recv_sem.at[2],
            device_id=(mx, below), device_id_type=MESH),
    ]
    copies[0].start()
    for x in range(8):
        low_ref[x] = jnp.dot(basis_ref[2 * x], held[x, 0], preferred_element_type=F32).astype(BF16)
        if x == 0:
            copies[1].start()
    copies[2].start()
    for x in range(8):
        up_ref[x] = jnp.dot(basis_ref[2 * x + 1], held[x, 1], preferred_element_type=F32).astype(BF16)

    def store(p, value):
        coarse_ref[p] = value

    sums = (jnp.ones((8, 128), F32), jnp.zeros((8, 128), F32))
    north_east = [basis_ref[4 * p] for p in range(4)] + [basis_ref[4 * p + 3] for p in range(4)]
    north_west = [basis_ref[4 * p + 2] for p in range(4)] + [basis_ref[4 * p + 5] for p in range(3)]
    low_sides = pair_sides(spread(north_east), spread(north_west + north_west[:1]))
    sides = high_sides([up_ref[2 * p] for p in range(4)], [up_ref[2 * p + 1] for p in range(4)])
    ahead = low_pair(low_sides, 0), high_pair(sides, 0)
    for p in range(4):
        (low, high), ahead = ahead, (low_pair(low_sides, p + 1), high_pair(sides, p + 1)) if p < 3 else None
        sums = finish(0, p, low, high, sums, store)
    for p in range(3):
        lows_ref[p] = low_pair(low_sides, p + 4)
    sums_ref[0] = sums[0]
    sums_ref[1] = sums[1]
    last_ref[0] = basis_ref[15]
    for copy in copies:
        copy.wait()
    last_ref[1] = halo_basis[0]
    halo_ref[...] = halo_second[...]


def join_kernel(
    first_ref, sums_ref, lows_ref, last_ref, halo_ref, coarse_ref, log_ref, trace_ref,
    stage, log_stage, trace_stage, out_sem,
):
    early = [pltpu.make_async_copy(first_ref.at[p], coarse_ref.at[p, 0], out_sem.at[p]) for p in range(4)]
    late = [pltpu.make_async_copy(stage.at[p], coarse_ref.at[p, 1], out_sem.at[4 + p]) for p in range(4)]
    small = [
        pltpu.make_async_copy(log_stage, log_ref, out_sem.at[8]),
        pltpu.make_async_copy(trace_stage, trace_ref, out_sem.at[9]),
    ]
    for copy in early:
        copy.start()

    def store(p, value):
        stage[p] = value
        late[p].start()

    sides = high_sides([halo_ref[2 * p] for p in range(4)], [halo_ref[2 * p + 1] for p in range(4)])
    edge = spread([last_ref[0], last_ref[1]] + [last_ref[0]] * 6)
    last_sides = pair_sides(edge, pltpu.roll(edge, HALF - CHI, 1))
    sums = (sums_ref[0], sums_ref[1])
    ahead = lows_ref[0], high_pair(sides, 0)
    for p in range(4):
        low, high = ahead
        if p < 3:
            ahead = lows_ref[p + 1] if p < 2 else low_pair(last_sides, 0), high_pair(sides, p + 1)
        sums = finish(1, p, low, high, sums, store)
    squares, traces = sums
    norm = jnp.sqrt(squares)
    log_stage[...] = jnp.log(norm)[:2, :4]
    trace_stage[...] = (CHI * traces / norm)[:2, :4]
    for copy in small:
        copy.start()
    for copy in early + late + small:
        copy.wait()


def solution(mesh):
    nx, ny = mesh.shape["gx"], mesh.shape["gy"]
    vmem = pl.BlockSpec(memory_space=pltpu.VMEM)
    hbm = pl.BlockSpec(memory_space=pltpu.HBM)

    def body(site_tensors, test_matrix):
        site_tensors = pltpu.with_memory_space_constraint(site_tensors, pltpu.HBM)
        test_matrix = pltpu.with_memory_space_constraint(test_matrix, pltpu.HBM)
        between = pl.pallas_call(
            lambda *refs: split_kernel(nx, ny, *refs),
            out_shape=(
                pltpu.VMEM((4, WIDE, WIDE), BF16),
                pltpu.VMEM((2, 8, 128), F32),
                pltpu.VMEM((3, WIDE, WIDE), BF16),
                pltpu.VMEM((2, CHI, WIDE), BF16),
                pltpu.VMEM((8, CHI, WIDE), BF16),
            ),
            in_specs=[hbm, hbm],
            out_specs=(vmem,) * 5,
            scratch_shapes=[
                pltpu.VMEM((8, 2, WIDE, WIDE), BF16),
                pltpu.VMEM((16, CHI, WIDE), BF16),
                pltpu.VMEM((8, CHI, WIDE), BF16),
                pltpu.VMEM((8, CHI, WIDE), BF16),
                pltpu.VMEM((1, CHI, WIDE), BF16),
                pltpu.VMEM((8, CHI, WIDE), BF16),
                pltpu.VMEM((8, 2, CHI, WIDE), BF16),
                pltpu.SemaphoreType.DMA((9,)),
                pltpu.SemaphoreType.DMA((3,)),
                pltpu.SemaphoreType.DMA((3,)),
            ],
            compiler_params=pltpu.CompilerParams(
                collective_id=0, has_side_effects=True, vmem_limit_bytes=24 * 2**20),
            cost_estimate=pl.CostEstimate(
                flops=700_000_000, bytes_accessed=3_000_000, transcendentals=0),
        )(site_tensors, test_matrix)
        between = [pltpu.with_memory_space_constraint(x, pltpu.VMEM) for x in between]
        coarse, log_norm, trace = pl.pallas_call(
            join_kernel,
            out_shape=(
                pltpu.HBM((4, 2, WIDE, WIDE), BF16),
                pltpu.HBM((2, 4), F32),
                pltpu.HBM((2, 4), F32),
            ),
            in_specs=[vmem] * 5,
            out_specs=(hbm, hbm, hbm),
            scratch_shapes=[
                pltpu.VMEM((4, WIDE, WIDE), BF16),
                pltpu.VMEM((2, 4), F32),
                pltpu.VMEM((2, 4), F32),
                pltpu.SemaphoreType.DMA((10,)),
            ],
            compiler_params=pltpu.CompilerParams(vmem_limit_bytes=24 * 2**20),
            cost_estimate=pl.CostEstimate(
                flops=300_000_000, bytes_accessed=1_000_000, transcendentals=0),
        )(*between)
        return coarse, log_norm.T, trace.T

    in_specs = (P("gx", "gy", None, None), P("gx", "gy", None, None))
    out_specs = (P("gx", "gy", None, None), P("gx", "gy"), P("gx", "gy"))
    return jax.shard_map(body, mesh=mesh, in_specs=in_specs, out_specs=out_specs, check_vma=False)
```

```python
import jax
import jax.numpy as jnp
from jax import lax
from jax.experimental import pallas as pl
from jax.experimental.pallas import tpu as pltpu
from jax.sharding import PartitionSpec as P

CHI = 16
WIDE = CHI * CHI
HALF = WIDE // 2
MESH = pl.DeviceIdType.MESH
F32 = jnp.float32
BF16 = jnp.bfloat16
NT = (((1,), (1,)), ((), ()))
NN = (((1,), (0,)), ((), ()))


def iota(shape, axis):
    return lax.broadcasted_iota(jnp.int32, shape, axis)


def swap_chunks(rows):
    rows = list(rows)
    chunk = iota(rows[0].shape, 1) // CHI
    for step in (4, 2, 1):
        low = (chunk & step) == 0
        for i in range(8):
            if i & step:
                continue
            first, other = rows[i], rows[i + step]
            if step == 4:
                moved = pltpu.roll(jnp.where(low, other, first), HALF // 2, 1)
                rows[i], rows[i + step] = jnp.where(low, first, moved), jnp.where(low, moved, other)
                continue
            rows[i] = jnp.where(low, first, pltpu.roll(other, CHI * step, 1))
            rows[i + step] = jnp.where(low, pltpu.roll(first, HALF - CHI * step, 1), other)
    return rows


def spread(halves):
    parts = []
    for side in range(2):
        parts += swap_chunks([h[:, side * HALF:(side + 1) * HALF] for h in halves])
    return jnp.concatenate(parts, axis=0)


def regroup(x):
    columns = []
    for upper in range(2):
        column = []
        for side in range(2):
            column += swap_chunks([
                x[(upper * 8 + v) * CHI:(upper * 8 + v + 1) * CHI, side * HALF:(side + 1) * HALF]
                for v in range(8)
            ])
        columns.append(jnp.concatenate(column, axis=0))
    return jnp.concatenate(columns, axis=1)


def eliminate(grams):
    row = iota(grams[0].shape, 0)
    lane = iota(grams[0].shape, 1)
    grams = list(grams)
    inverses = [jnp.where(row == lane % CHI, 1.0, 0.0).astype(F32)] * len(grams)
    pivots = list(grams)
    for k in range(0, CHI, 2):
        for s in range(len(grams)):
            gram, inverse = grams[s], inverses[s]
            first = jnp.take_along_axis(gram, lane // CHI * CHI + k, axis=1)
            second = jnp.take_along_axis(gram, lane // CHI * CHI + k + 1, axis=1)
            over = 1.0 / first[k:k + 1]
            first_factor = first * over
            shared = second[k:k + 1]
            second = second - first_factor * shared
            step = first_factor[k + 1:k + 2]
            gram_row, inverse_row = gram[k:k + 1], inverse[k:k + 1]
            gram_next = gram[k + 1:k + 2] - step * gram_row
            inverse_next = inverse[k + 1:k + 2] - step * inverse_row
            pivots[s] = jnp.where(row == k, first[k:k + 1], jnp.where(row == k + 1, second[k + 1:k + 2], pivots[s]))
            first_factor = jnp.where(row > k, first_factor, 0.0)
            second_factor = jnp.where(row > k + 1, second * (1.0 / second[k + 1:k + 2]), 0.0)
            grams[s] = gram - first_factor * gram_row - second_factor * gram_next
            inverses[s] = inverse - first_factor * inverse_row - second_factor * inverse_next
    return [i * lax.rsqrt(p) for i, p in zip(inverses, pivots)]


def flip_mask():
    row, col = iota((WIDE, WIDE), 0), iota((WIDE, WIDE), 1)
    return jnp.where((row // CHI == col % CHI) & (row % CHI == col // CHI), 1.0, 0.0).astype(F32)


def pair_sides(left, right):
    left = jnp.dot(flip_mask().astype(BF16), left, preferred_element_type=F32).astype(BF16)
    return left, right, left.T, right.T


def low_pair(sides, q):
    chunk = iota((WIDE, HALF), 1) // CHI
    masked = jnp.where(chunk == q, sides[1], jnp.zeros((), BF16))
    return regroup(jnp.dot(masked, sides[2], preferred_element_type=F32).astype(BF16))


def high_pair(sides, q):
    chunk = iota((WIDE, HALF), 1) // CHI
    masked = jnp.where(chunk == q, sides[0], jnp.zeros((), BF16))
    return regroup(jnp.dot(masked, sides[3], preferred_element_type=F32).astype(BF16))


def high_sides(south_east, south_west):
    turned = jnp.dot(
        jnp.concatenate(south_east, axis=0), flip_mask().astype(BF16), preferred_element_type=F32).astype(BF16)
    both = spread([turned[q * CHI:(q + 1) * CHI] for q in range(4)] + south_west)
    return pair_sides(both, pltpu.roll(both, HALF // 2, 1))


def finish(g, p, low, high, sums, store):
    squares, traces = sums
    raw = jnp.dot(low, high, preferred_element_type=F32)
    square = jnp.sum(jnp.sum(raw * raw, axis=0, keepdims=True), axis=1, keepdims=True) + 1e-6
    traced = jnp.sum(jnp.sum(raw * flip_mask(), axis=0, keepdims=True), axis=1, keepdims=True)
    store(p, (raw * (WIDE * lax.rsqrt(square))).astype(BF16))
    here = (iota((8, 128), 0) == g) & (iota((8, 128), 1) == p)
    return jnp.where(here, square, squares), jnp.where(here, traced, traces)


def split_kernel(
    nx, ny, tensors_ref, tests_ref, coarse_ref, sums_ref, lows_ref, last_ref, halo_ref,
    held, basis_ref, low_ref, up_ref, halo_basis, halo_second, tests, in_sem, send_sem, recv_sem,
):
    mx, my = lax.axis_index("gx"), lax.axis_index("gy")
    right, left = lax.rem(mx + 1, nx), lax.rem(mx + nx - 1, nx)
    above, below = lax.rem(my + 1, ny), lax.rem(my + ny - 1, ny)
    loads = [pltpu.make_async_copy(tensors_ref.at[c], held.at[c], in_sem.at[c]) for c in range(8)]
    loads.append(pltpu.make_async_copy(tests_ref, tests, in_sem.at[8]))
    loads[8].start()
    for load in loads[:8]:
        load.start()
    barrier = pltpu.get_barrier_semaphore()
    for target in ((right, my), (mx, above), (right, above)):
        pl.semaphore_signal(barrier, inc=1, device_id=target, device_id_type=MESH)

    sketches = []
    loads[8].wait()
    for x in range(8):
        loads[x].wait()
        for y in range(2):
            sketches.append(lax.dot_general(tests[x, y], held[x, y], NT, preferred_element_type=F32))
    sketch = jnp.concatenate(sketches, axis=0)
    chunk = iota((CHI, HALF), 1) // CHI
    grams = []
    for side in range(2):
        part = sketch[side * HALF:(side + 1) * HALF]
        product = lax.dot_general(part, part, NT, precision=lax.Precision.HIGHEST, preferred_element_type=F32)
        gram = jnp.zeros((CHI, HALF), F32)
        for n in range(8):
            gram = gram + jnp.where(chunk == n, product[n * CHI:(n + 1) * CHI], 0.0)
        grams.append(gram)
    for side, inverse in enumerate(eliminate(grams)):
        part = sketch[side * HALF:(side + 1) * HALF]
        block = jnp.concatenate([jnp.where(chunk == n, inverse, 0.0) for n in range(8)], axis=0)
        basis = lax.dot_general(block, part, NN, precision=lax.Precision.HIGHEST, preferred_element_type=F32)
        basis_ref[pl.ds(8 * side, 8)] = basis.astype(BF16).reshape(8, CHI, WIDE)

    copies = [
        pltpu.make_async_remote_copy(
            basis_ref.at[1], halo_basis.at[0], send_sem.at[0], recv_sem.at[0],
            device_id=(left, my), device_id_type=MESH),
        pltpu.make_async_remote_copy(
            low_ref.at[0], halo_second.at[7], send_sem.at[1], recv_sem.at[1],
            device_id=(left, below), device_id_type=MESH),
        pltpu.make_async_remote_copy(
            low_ref.at[pl.ds(1, 7)], halo_second.at[pl.ds(0, 7)], send_sem.at[2], recv_sem.at[2],
            device_id=(mx, below), device_id_type=MESH),
    ]
    def send():
        pl.semaphore_wait(barrier, 3)
        for copy in copies:
            copy.start()

    for x in range(8):
        low_ref[x] = jnp.dot(basis_ref[2 * x], held[x, 0], preferred_element_type=F32).astype(BF16)
    pl.when(my != 0)(send)
    for x in range(8):
        up_ref[x] = jnp.dot(basis_ref[2 * x + 1], held[x, 1], preferred_element_type=F32).astype(BF16)

    def store(p, value):
        coarse_ref[p] = value

    sums = (jnp.ones((8, 128), F32), jnp.zeros((8, 128), F32))
    north_east = [basis_ref[4 * p] for p in range(4)] + [basis_ref[4 * p + 3] for p in range(4)]
    north_west = [basis_ref[4 * p + 2] for p in range(4)] + [basis_ref[4 * p + 5] for p in range(3)]
    low_sides = pair_sides(spread(north_east), spread(north_west + north_west[:1]))
    sides = high_sides([up_ref[2 * p] for p in range(4)], [up_ref[2 * p + 1] for p in range(4)])
    ahead = low_pair(low_sides, 0), high_pair(sides, 0)
    for p in range(4):
        (low, high), ahead = ahead, (low_pair(low_sides, p + 1), high_pair(sides, p + 1)) if p < 3 else None
        sums = finish(0, p, low, high, sums, store)
    for p in range(3):
        lows_ref[p] = low_pair(low_sides, p + 4)
    sums_ref[0] = sums[0]
    sums_ref[1] = sums[1]
    last_ref[0] = basis_ref[15]
    pl.when(my == 0)(send)
    for copy in copies:
        copy.wait()
    last_ref[1] = halo_basis[0]
    halo_ref[...] = halo_second[...]


def join_kernel(
    first_ref, sums_ref, lows_ref, last_ref, halo_ref, coarse_ref, log_ref, trace_ref,
    stage, log_stage, trace_stage, out_sem,
):
    early = [pltpu.make_async_copy(first_ref.at[p], coarse_ref.at[p, 0], out_sem.at[p]) for p in range(4)]
    late = [pltpu.make_async_copy(stage.at[p], coarse_ref.at[p, 1], out_sem.at[4 + p]) for p in range(4)]
    small = [
        pltpu.make_async_copy(log_stage, log_ref, out_sem.at[8]),
        pltpu.make_async_copy(trace_stage, trace_ref, out_sem.at[9]),
    ]
    for copy in early:
        copy.start()

    def store(p, value):
        stage[p] = value
        late[p].start()

    sides = high_sides([halo_ref[2 * p] for p in range(4)], [halo_ref[2 * p + 1] for p in range(4)])
    edge = spread([last_ref[0], last_ref[1]] + [last_ref[0]] * 6)
    last_sides = pair_sides(edge, pltpu.roll(edge, HALF - CHI, 1))
    sums = (sums_ref[0], sums_ref[1])
    ahead = lows_ref[0], high_pair(sides, 0)
    for p in range(4):
        low, high = ahead
        if p < 3:
            ahead = lows_ref[p + 1] if p < 2 else low_pair(last_sides, 0), high_pair(sides, p + 1)
        sums = finish(1, p, low, high, sums, store)
    squares, traces = sums
    norm = jnp.sqrt(squares)
    log_stage[...] = jnp.log(norm)[:2, :4]
    trace_stage[...] = (CHI * traces / norm)[:2, :4]
    for copy in small:
        copy.start()
    for copy in early + late + small:
        copy.wait()


def solution(mesh):
    nx, ny = mesh.shape["gx"], mesh.shape["gy"]
    vmem = pl.BlockSpec(memory_space=pltpu.VMEM)
    hbm = pl.BlockSpec(memory_space=pltpu.HBM)

    def body(site_tensors, test_matrix):
        site_tensors = pltpu.with_memory_space_constraint(site_tensors, pltpu.HBM)
        test_matrix = pltpu.with_memory_space_constraint(test_matrix, pltpu.HBM)
        between = pl.pallas_call(
            lambda *refs: split_kernel(nx, ny, *refs),
            out_shape=(
                pltpu.VMEM((4, WIDE, WIDE), BF16),
                pltpu.VMEM((2, 8, 128), F32),
                pltpu.VMEM((3, WIDE, WIDE), BF16),
                pltpu.VMEM((2, CHI, WIDE), BF16),
                pltpu.VMEM((8, CHI, WIDE), BF16),
            ),
            in_specs=[hbm, hbm],
            out_specs=(vmem,) * 5,
            scratch_shapes=[
                pltpu.VMEM((8, 2, WIDE, WIDE), BF16),
                pltpu.VMEM((16, CHI, WIDE), BF16),
                pltpu.VMEM((8, CHI, WIDE), BF16),
                pltpu.VMEM((8, CHI, WIDE), BF16),
                pltpu.VMEM((1, CHI, WIDE), BF16),
                pltpu.VMEM((8, CHI, WIDE), BF16),
                pltpu.VMEM((8, 2, CHI, WIDE), BF16),
                pltpu.SemaphoreType.DMA((9,)),
                pltpu.SemaphoreType.DMA((3,)),
                pltpu.SemaphoreType.DMA((3,)),
            ],
            compiler_params=pltpu.CompilerParams(
                collective_id=0, has_side_effects=True, vmem_limit_bytes=24 * 2**20),
            cost_estimate=pl.CostEstimate(
                flops=700_000_000, bytes_accessed=3_000_000, transcendentals=0),
        )(site_tensors, test_matrix)
        between = [pltpu.with_memory_space_constraint(x, pltpu.VMEM) for x in between]
        coarse, log_norm, trace = pl.pallas_call(
            join_kernel,
            out_shape=(
                pltpu.HBM((4, 2, WIDE, WIDE), BF16),
                pltpu.HBM((2, 4), F32),
                pltpu.HBM((2, 4), F32),
            ),
            in_specs=[vmem] * 5,
            out_specs=(hbm, hbm, hbm),
            scratch_shapes=[
                pltpu.VMEM((4, WIDE, WIDE), BF16),
                pltpu.VMEM((2, 4), F32),
                pltpu.VMEM((2, 4), F32),
                pltpu.SemaphoreType.DMA((10,)),
            ],
            compiler_params=pltpu.CompilerParams(vmem_limit_bytes=24 * 2**20),
            cost_estimate=pl.CostEstimate(
                flops=300_000_000, bytes_accessed=1_000_000, transcendentals=0),
        )(*between)
        return coarse, log_norm.T, trace.T

    in_specs = (P("gx", "gy", None, None), P("gx", "gy", None, None))
    out_specs = (P("gx", "gy", None, None), P("gx", "gy"), P("gx", "gy"))
    return jax.shard_map(body, mesh=mesh, in_specs=in_specs, out_specs=out_specs, check_vma=False)
```

```python
import jax
import jax.numpy as jnp
from jax import lax
from jax.experimental import pallas as pl
from jax.experimental.pallas import tpu as pltpu
from jax.sharding import PartitionSpec as P

CHI = 16
WIDE = CHI * CHI
HALF = WIDE // 2
MESH = pl.DeviceIdType.MESH
F32 = jnp.float32
BF16 = jnp.bfloat16
NT = (((1,), (1,)), ((), ()))
NN = (((1,), (0,)), ((), ()))


def iota(shape, axis):
    return lax.broadcasted_iota(jnp.int32, shape, axis)


def swap_chunks(rows):
    rows = list(rows)
    chunk = iota(rows[0].shape, 1) // CHI
    for step in (4, 2, 1):
        low = (chunk & step) == 0
        for i in range(8):
            if i & step:
                continue
            first, other = rows[i], rows[i + step]
            if step == 4:
                moved = pltpu.roll(jnp.where(low, other, first), HALF // 2, 1)
                rows[i], rows[i + step] = jnp.where(low, first, moved), jnp.where(low, moved, other)
                continue
            rows[i] = jnp.where(low, first, pltpu.roll(other, CHI * step, 1))
            rows[i + step] = jnp.where(low, pltpu.roll(first, HALF - CHI * step, 1), other)
    return rows


def spread(halves):
    parts = []
    for side in range(2):
        parts += swap_chunks([h[:, side * HALF:(side + 1) * HALF] for h in halves])
    return jnp.concatenate(parts, axis=0)


def regroup(x):
    columns = []
    for upper in range(2):
        column = []
        for side in range(2):
            column += swap_chunks([
                x[(upper * 8 + v) * CHI:(upper * 8 + v + 1) * CHI, side * HALF:(side + 1) * HALF]
                for v in range(8)
            ])
        columns.append(jnp.concatenate(column, axis=0))
    return jnp.concatenate(columns, axis=1)


def eliminate(grams):
    row = iota(grams[0].shape, 0)
    lane = iota(grams[0].shape, 1)
    grams = list(grams)
    inverses = [jnp.where(row == lane % CHI, 1.0, 0.0).astype(F32)] * len(grams)
    pivots = list(grams)
    for k in range(0, CHI, 2):
        for s in range(len(grams)):
            gram, inverse = grams[s], inverses[s]
            first = jnp.take_along_axis(gram, lane // CHI * CHI + k, axis=1)
            second = jnp.take_along_axis(gram, lane // CHI * CHI + k + 1, axis=1)
            over = 1.0 / first[k:k + 1]
            first_factor = first * over
            shared = second[k:k + 1]
            second = second - first_factor * shared
            step = first_factor[k + 1:k + 2]
            gram_row, inverse_row = gram[k:k + 1], inverse[k:k + 1]
            gram_next = gram[k + 1:k + 2] - step * gram_row
            inverse_next = inverse[k + 1:k + 2] - step * inverse_row
            pivots[s] = jnp.where(row == k, first[k:k + 1], jnp.where(row == k + 1, second[k + 1:k + 2], pivots[s]))
            first_factor = jnp.where(row > k, first_factor, 0.0)
            second_factor = jnp.where(row > k + 1, second * (1.0 / second[k + 1:k + 2]), 0.0)
            grams[s] = gram - first_factor * gram_row - second_factor * gram_next
            inverses[s] = inverse - first_factor * inverse_row - second_factor * inverse_next
    return [i * lax.rsqrt(p) for i, p in zip(inverses, pivots)]


def flip_mask():
    row, col = iota((WIDE, WIDE), 0), iota((WIDE, WIDE), 1)
    return jnp.where((row // CHI == col % CHI) & (row % CHI == col // CHI), 1.0, 0.0).astype(F32)


def pair_sides(left, right):
    left = jnp.dot(flip_mask().astype(BF16), left, preferred_element_type=F32).astype(BF16)
    return left, right, left.T, right.T


def low_pair(sides, q):
    chunk = iota((WIDE, HALF), 1) // CHI
    masked = jnp.where(chunk == q, sides[1], jnp.zeros((), BF16))
    return regroup(jnp.dot(masked, sides[2], preferred_element_type=F32).astype(BF16))


def high_pair(sides, q):
    chunk = iota((WIDE, HALF), 1) // CHI
    masked = jnp.where(chunk == q, sides[0], jnp.zeros((), BF16))
    return regroup(jnp.dot(masked, sides[3], preferred_element_type=F32).astype(BF16))


def high_sides(south_east, south_west):
    turned = jnp.dot(
        jnp.concatenate(south_east, axis=0), flip_mask().astype(BF16), preferred_element_type=F32).astype(BF16)
    both = spread([turned[q * CHI:(q + 1) * CHI] for q in range(4)] + south_west)
    return pair_sides(both, pltpu.roll(both, HALF // 2, 1))


def finish(g, p, low, high, sums, store):
    squares, traces = sums
    raw = jnp.dot(low, high, preferred_element_type=F32)
    square = jnp.sum(jnp.sum(raw * raw, axis=0, keepdims=True), axis=1, keepdims=True) + 1e-6
    traced = jnp.sum(jnp.sum(raw * flip_mask(), axis=0, keepdims=True), axis=1, keepdims=True)
    store(p, (raw * (WIDE * lax.rsqrt(square))).astype(BF16))
    here = (iota((8, 128), 0) == g) & (iota((8, 128), 1) == p)
    return jnp.where(here, square, squares), jnp.where(here, traced, traces)


def split_kernel(
    nx, ny, tensors_ref, tests_ref, coarse_ref, sums_ref, lows_ref, last_ref, halo_ref,
    held, basis_ref, low_ref, up_ref, halo_basis, halo_second, tests, in_sem, send_sem, recv_sem,
):
    mx, my = lax.axis_index("gx"), lax.axis_index("gy")
    right, left = lax.rem(mx + 1, nx), lax.rem(mx + nx - 1, nx)
    above, below = lax.rem(my + 1, ny), lax.rem(my + ny - 1, ny)
    loads = [pltpu.make_async_copy(tensors_ref.at[c], held.at[c], in_sem.at[c]) for c in range(8)]
    loads.append(pltpu.make_async_copy(tests_ref, tests, in_sem.at[8]))
    loads[8].start()
    for load in loads[:8]:
        load.start()
    barrier = pltpu.get_barrier_semaphore()
    for target in ((right, my), (mx, above), (right, above)):
        pl.semaphore_signal(barrier, inc=1, device_id=target, device_id_type=MESH)

    loads[8].wait()
    chunk = iota((CHI, HALF), 1) // CHI
    tall = iota((WIDE, HALF), 1) // CHI
    parts, grams = [], []
    for side in range(2):
        across = jnp.concatenate([tests[4 * side + n // 2, n % 2] for n in range(8)], axis=0).T
        sketch = None
        for n in range(8):
            x, y = 4 * side + n // 2, n % 2
            if y == 0:
                loads[x].wait()
            wide = jnp.dot(held[x, y], across, preferred_element_type=F32)
            sketch = wide if n == 0 else jnp.where(tall == n, wide, sketch)
        part = sketch.T
        product = jnp.dot(part, sketch, precision=lax.Precision.HIGHEST, preferred_element_type=F32)
        gram = product[:CHI]
        for n in range(1, 8):
            gram = jnp.where(chunk == n, product[n * CHI:(n + 1) * CHI], gram)
        parts.append(part)
        grams.append(gram)
    for side, inverse in enumerate(eliminate(grams)):
        block = jnp.concatenate([jnp.where(chunk == n, inverse, 0.0) for n in range(8)], axis=0)
        basis = jnp.dot(block, parts[side], precision=lax.Precision.HIGHEST, preferred_element_type=F32)
        basis_ref[pl.ds(8 * side, 8)] = basis.astype(BF16).reshape(8, CHI, WIDE)

    copies = [
        pltpu.make_async_remote_copy(
            basis_ref.at[1], halo_basis.at[0], send_sem.at[0], recv_sem.at[0],
            device_id=(left, my), device_id_type=MESH),
        pltpu.make_async_remote_copy(
            low_ref.at[0], halo_second.at[7], send_sem.at[1], recv_sem.at[1],
            device_id=(left, below), device_id_type=MESH),
        pltpu.make_async_remote_copy(
            low_ref.at[pl.ds(1, 7)], halo_second.at[pl.ds(0, 7)], send_sem.at[2], recv_sem.at[2],
            device_id=(mx, below), device_id_type=MESH),
    ]
    def send():
        pl.semaphore_wait(barrier, 3)
        for copy in copies:
            copy.start()

    for x in range(8):
        low_ref[x] = jnp.dot(basis_ref[2 * x], held[x, 0], preferred_element_type=F32).astype(BF16)
    first_chip = (my == 0) & (mx < 2)
    pl.when(jnp.logical_not(first_chip))(send)
    for x in range(8):
        up_ref[x] = jnp.dot(basis_ref[2 * x + 1], held[x, 1], preferred_element_type=F32).astype(BF16)

    def store(p, value):
        coarse_ref[p] = value

    sums = (jnp.ones((8, 128), F32), jnp.zeros((8, 128), F32))
    north_east = [basis_ref[4 * p] for p in range(4)] + [basis_ref[4 * p + 3] for p in range(4)]
    north_west = [basis_ref[4 * p + 2] for p in range(4)] + [basis_ref[4 * p + 5] for p in range(3)]
    low_sides = pair_sides(spread(north_east), spread(north_west + north_west[:1]))
    sides = high_sides([up_ref[2 * p] for p in range(4)], [up_ref[2 * p + 1] for p in range(4)])
    for p in range(3):
        lows_ref[p] = low_pair(low_sides, p + 4)
    ahead = low_pair(low_sides, 0), high_pair(sides, 0)
    pl.when(first_chip)(send)
    for p in range(4):
        (low, high), ahead = ahead, (low_pair(low_sides, p + 1), high_pair(sides, p + 1)) if p < 3 else None
        sums = finish(0, p, low, high, sums, store)
    sums_ref[0] = sums[0]
    sums_ref[1] = sums[1]
    last_ref[0] = basis_ref[15]
    for copy in copies:
        copy.wait()
    last_ref[1] = halo_basis[0]
    halo_ref[...] = halo_second[...]


def join_kernel(
    first_ref, sums_ref, lows_ref, last_ref, halo_ref, coarse_ref, log_ref, trace_ref,
    stage, log_stage, trace_stage, out_sem,
):
    early = [pltpu.make_async_copy(first_ref.at[p], coarse_ref.at[p, 0], out_sem.at[p]) for p in range(4)]
    late = [pltpu.make_async_copy(stage.at[p], coarse_ref.at[p, 1], out_sem.at[4 + p]) for p in range(4)]
    small = [
        pltpu.make_async_copy(log_stage, log_ref, out_sem.at[8]),
        pltpu.make_async_copy(trace_stage, trace_ref, out_sem.at[9]),
    ]
    for copy in early:
        copy.start()

    def store(p, value):
        stage[p] = value
        late[p].start()

    sides = high_sides([halo_ref[2 * p] for p in range(4)], [halo_ref[2 * p + 1] for p in range(4)])
    edge = spread([last_ref[0], last_ref[1]] + [last_ref[0]] * 6)
    last_sides = pair_sides(edge, pltpu.roll(edge, HALF - CHI, 1))
    sums = (sums_ref[0], sums_ref[1])
    ahead = lows_ref[0], high_pair(sides, 0)
    for p in range(4):
        low, high = ahead
        if p < 3:
            ahead = lows_ref[p + 1] if p < 2 else low_pair(last_sides, 0), high_pair(sides, p + 1)
        sums = finish(1, p, low, high, sums, store)
    squares, traces = sums
    norm = jnp.sqrt(squares)
    log_stage[...] = jnp.log(norm)[:2, :4]
    trace_stage[...] = (CHI * traces / norm)[:2, :4]
    for copy in small:
        copy.start()
    for copy in early + late + small:
        copy.wait()


def solution(mesh):
    nx, ny = mesh.shape["gx"], mesh.shape["gy"]
    vmem = pl.BlockSpec(memory_space=pltpu.VMEM)
    hbm = pl.BlockSpec(memory_space=pltpu.HBM)

    def body(site_tensors, test_matrix):
        site_tensors = pltpu.with_memory_space_constraint(site_tensors, pltpu.HBM)
        test_matrix = pltpu.with_memory_space_constraint(test_matrix, pltpu.HBM)
        between = pl.pallas_call(
            lambda *refs: split_kernel(nx, ny, *refs),
            out_shape=(
                pltpu.VMEM((4, WIDE, WIDE), BF16),
                pltpu.VMEM((2, 8, 128), F32),
                pltpu.VMEM((3, WIDE, WIDE), BF16),
                pltpu.VMEM((2, CHI, WIDE), BF16),
                pltpu.VMEM((8, CHI, WIDE), BF16),
            ),
            in_specs=[hbm, hbm],
            out_specs=(vmem,) * 5,
            scratch_shapes=[
                pltpu.VMEM((8, 2, WIDE, WIDE), BF16),
                pltpu.VMEM((16, CHI, WIDE), BF16),
                pltpu.VMEM((8, CHI, WIDE), BF16),
                pltpu.VMEM((8, CHI, WIDE), BF16),
                pltpu.VMEM((1, CHI, WIDE), BF16),
                pltpu.VMEM((8, CHI, WIDE), BF16),
                pltpu.VMEM((8, 2, CHI, WIDE), BF16),
                pltpu.SemaphoreType.DMA((9,)),
                pltpu.SemaphoreType.DMA((3,)),
                pltpu.SemaphoreType.DMA((3,)),
            ],
            compiler_params=pltpu.CompilerParams(
                collective_id=0, has_side_effects=True, vmem_limit_bytes=24 * 2**20),
            cost_estimate=pl.CostEstimate(
                flops=700_000_000, bytes_accessed=3_000_000, transcendentals=0),
        )(site_tensors, test_matrix)
        between = [pltpu.with_memory_space_constraint(x, pltpu.VMEM) for x in between]
        coarse, log_norm, trace = pl.pallas_call(
            join_kernel,
            out_shape=(
                pltpu.HBM((4, 2, WIDE, WIDE), BF16),
                pltpu.HBM((2, 4), F32),
                pltpu.HBM((2, 4), F32),
            ),
            in_specs=[vmem] * 5,
            out_specs=(hbm, hbm, hbm),
            scratch_shapes=[
                pltpu.VMEM((4, WIDE, WIDE), BF16),
                pltpu.VMEM((2, 4), F32),
                pltpu.VMEM((2, 4), F32),
                pltpu.SemaphoreType.DMA((10,)),
            ],
            compiler_params=pltpu.CompilerParams(vmem_limit_bytes=24 * 2**20),
            cost_estimate=pl.CostEstimate(
                flops=300_000_000, bytes_accessed=1_000_000, transcendentals=0),
        )(*between)
        return coarse, log_norm.T, trace.T

    in_specs = (P("gx", "gy", None, None), P("gx", "gy", None, None))
    out_specs = (P("gx", "gy", None, None), P("gx", "gy"), P("gx", "gy"))
    return jax.shard_map(body, mesh=mesh, in_specs=in_specs, out_specs=out_specs, check_vma=False)
```

```python
import jax
import jax.numpy as jnp
from jax import lax
from jax.experimental import pallas as pl
from jax.experimental.pallas import tpu as pltpu
from jax.sharding import PartitionSpec as P

CHI = 16
WIDE = CHI * CHI
HALF = WIDE // 2
MESH = pl.DeviceIdType.MESH
F32 = jnp.float32
BF16 = jnp.bfloat16
NT = (((1,), (1,)), ((), ()))
NN = (((1,), (0,)), ((), ()))


def iota(shape, axis):
    return lax.broadcasted_iota(jnp.int32, shape, axis)


def swap_chunks(rows):
    rows = list(rows)
    chunk = iota(rows[0].shape, 1) // CHI
    for step in (4, 2, 1):
        low = (chunk & step) == 0
        for i in range(8):
            if i & step:
                continue
            first, other = rows[i], rows[i + step]
            if step == 4:
                moved = pltpu.roll(jnp.where(low, other, first), HALF // 2, 1)
                rows[i], rows[i + step] = jnp.where(low, first, moved), jnp.where(low, moved, other)
                continue
            rows[i] = jnp.where(low, first, pltpu.roll(other, CHI * step, 1))
            rows[i + step] = jnp.where(low, pltpu.roll(first, HALF - CHI * step, 1), other)
    return rows


def spread(halves):
    parts = []
    for side in range(2):
        parts += swap_chunks([h[:, side * HALF:(side + 1) * HALF] for h in halves])
    return jnp.concatenate(parts, axis=0)


def regroup(x):
    columns = []
    for upper in range(2):
        column = []
        for side in range(2):
            column += swap_chunks([
                x[(upper * 8 + v) * CHI:(upper * 8 + v + 1) * CHI, side * HALF:(side + 1) * HALF]
                for v in range(8)
            ])
        columns.append(jnp.concatenate(column, axis=0))
    return jnp.concatenate(columns, axis=1)


def eliminate(grams):
    row = iota(grams[0].shape, 0)
    lane = iota(grams[0].shape, 1)
    grams = list(grams)
    inverses = [jnp.where(row == lane % CHI, 1.0, 0.0).astype(F32)] * len(grams)
    pivots = list(grams)
    for k in range(0, CHI, 2):
        for s in range(len(grams)):
            gram, inverse = grams[s], inverses[s]
            first = jnp.take_along_axis(gram, lane // CHI * CHI + k, axis=1)
            second = jnp.take_along_axis(gram, lane // CHI * CHI + k + 1, axis=1)
            over = 1.0 / first[k:k + 1]
            first_factor = first * over
            shared = second[k:k + 1]
            second = second - first_factor * shared
            step = first_factor[k + 1:k + 2]
            gram_row, inverse_row = gram[k:k + 1], inverse[k:k + 1]
            gram_next = gram[k + 1:k + 2] - step * gram_row
            inverse_next = inverse[k + 1:k + 2] - step * inverse_row
            pivots[s] = jnp.where(row == k, first[k:k + 1], jnp.where(row == k + 1, second[k + 1:k + 2], pivots[s]))
            first_factor = jnp.where(row > k, first_factor, 0.0)
            second_factor = jnp.where(row > k + 1, second * (1.0 / second[k + 1:k + 2]), 0.0)
            grams[s] = gram - first_factor * gram_row - second_factor * gram_next
            inverses[s] = inverse - first_factor * inverse_row - second_factor * inverse_next
    return [i * lax.rsqrt(p) for i, p in zip(inverses, pivots)]


def flip_mask():
    row, col = iota((WIDE, WIDE), 0), iota((WIDE, WIDE), 1)
    return jnp.where((row // CHI == col % CHI) & (row % CHI == col // CHI), 1.0, 0.0).astype(F32)


def pair_sides(left, right):
    left = jnp.dot(flip_mask().astype(BF16), left, preferred_element_type=F32).astype(BF16)
    return left, right, left.T, right.T


def low_pair(sides, q):
    chunk = iota((WIDE, HALF), 1) // CHI
    masked = jnp.where(chunk == q, sides[1], jnp.zeros((), BF16))
    return regroup(jnp.dot(masked, sides[2], preferred_element_type=F32).astype(BF16))


def high_pair(sides, q):
    chunk = iota((WIDE, HALF), 1) // CHI
    masked = jnp.where(chunk == q, sides[0], jnp.zeros((), BF16))
    return regroup(jnp.dot(masked, sides[3], preferred_element_type=F32).astype(BF16))


def high_sides(south_east, south_west):
    turned = jnp.dot(
        jnp.concatenate(south_east, axis=0), flip_mask().astype(BF16), preferred_element_type=F32).astype(BF16)
    both = spread([turned[q * CHI:(q + 1) * CHI] for q in range(4)] + south_west)
    return pair_sides(both, pltpu.roll(both, HALF // 2, 1))


def finish(g, p, low, high, sums, store):
    squares, traces = sums
    raw = jnp.dot(low, high, preferred_element_type=F32)
    square = jnp.sum(jnp.sum(raw * raw, axis=0, keepdims=True), axis=1, keepdims=True) + 1e-6
    traced = jnp.sum(jnp.sum(raw * flip_mask(), axis=0, keepdims=True), axis=1, keepdims=True)
    store(p, (raw * (WIDE * lax.rsqrt(square))).astype(BF16))
    here = (iota((8, 128), 0) == g) & (iota((8, 128), 1) == p)
    return jnp.where(here, square, squares), jnp.where(here, traced, traces)


def split_kernel(
    nx, ny, tensors_ref, tests_ref, coarse_ref, sums_ref, lows_ref, last_ref, halo_ref,
    held, basis_ref, low_ref, up_ref, halo_basis, halo_second, tests, own_lows, in_sem, send_sem, recv_sem,
):
    mx, my = lax.axis_index("gx"), lax.axis_index("gy")
    right, left = lax.rem(mx + 1, nx), lax.rem(mx + nx - 1, nx)
    above, below = lax.rem(my + 1, ny), lax.rem(my + ny - 1, ny)
    loads = [
        pltpu.make_async_copy(
            tensors_ref.at[pl.ds(2 * c, 2), y], held.at[y, pl.ds(2 * c, 2)], in_sem.at[4 * y + c])
        for y in range(2) for c in range(4)
    ]
    loads.append(pltpu.make_async_copy(tests_ref, tests, in_sem.at[8]))
    loads[8].start()
    for load in loads[:8]:
        load.start()
    barrier = pltpu.get_barrier_semaphore()
    for target in ((right, my), (mx, above), (right, above)):
        pl.semaphore_signal(barrier, inc=1, device_id=target, device_id_type=MESH)

    loads[8].wait()
    chunk = iota((CHI, HALF), 1) // CHI

    def sketch_row(y):
        sketches = []
        for x in range(8):
            if x % 2 == 0:
                loads[4 * y + x // 2].wait()
            sketches.append(lax.dot_general(tests[x, y], held[y, x], NT, preferred_element_type=F32))
        part = jnp.concatenate(sketches, axis=0)
        product = lax.dot_general(part, part, NT, precision=lax.Precision.HIGHEST, preferred_element_type=F32)
        gram = product[:CHI]
        for n in range(1, 8):
            gram = jnp.where(chunk == n, product[n * CHI:(n + 1) * CHI], gram)
        return part, gram

    def basis_row(y, part, gram):
        inverse = eliminate([gram])[0]
        block = jnp.concatenate([jnp.where(chunk == n, inverse, 0.0) for n in range(8)], axis=0)
        basis = jnp.dot(block, part, precision=lax.Precision.HIGHEST, preferred_element_type=F32)
        basis_ref[y] = basis.astype(BF16).reshape(8, CHI, WIDE)

    copies = [
        pltpu.make_async_remote_copy(
            basis_ref.at[1, 0], halo_basis.at[0], send_sem.at[0], recv_sem.at[0],
            device_id=(left, my), device_id_type=MESH),
        pltpu.make_async_remote_copy(
            low_ref.at[0], halo_second.at[7], send_sem.at[1], recv_sem.at[1],
            device_id=(left, below), device_id_type=MESH),
        pltpu.make_async_remote_copy(
            low_ref.at[pl.ds(1, 7)], halo_second.at[pl.ds(0, 7)], send_sem.at[2], recv_sem.at[2],
            device_id=(mx, below), device_id_type=MESH),
    ]
    def send_seconds():
        pl.semaphore_wait(barrier, 3)
        copies[1].start()
        copies[2].start()

    lower = sketch_row(0)
    upper = sketch_row(1)
    basis_row(0, *lower)
    for x in range(8):
        low_ref[x] = jnp.dot(basis_ref[0, x], held[0, x], preferred_element_type=F32).astype(BF16)
    first_chip = (my == 0) & (mx < 2)
    pl.when(jnp.logical_not(first_chip))(send_seconds)
    basis_row(1, *upper)
    both = spread([basis_ref[0, 2 * p] for p in range(4)] + [basis_ref[0, 2 * p + 1] for p in range(4)])
    low_sides = pair_sides(both, pltpu.roll(both, HALF // 2, 1))
    for p in range(4):
        own_lows[p] = low_pair(low_sides, p)
    pl.when(first_chip)(send_seconds)
    copies[0].start()
    for x in range(8):
        up_ref[x] = jnp.dot(basis_ref[1, x], held[1, x], preferred_element_type=F32).astype(BF16)

    def store(p, value):
        coarse_ref[p] = value

    sums = (jnp.ones((8, 128), F32), jnp.zeros((8, 128), F32))
    sides = high_sides([up_ref[2 * p] for p in range(4)], [up_ref[2 * p + 1] for p in range(4)])
    both = spread([basis_ref[1, 2 * p + 1] for p in range(4)] + [basis_ref[1, (2 * p + 2) % 8] for p in range(4)])
    low_sides = pair_sides(both, pltpu.roll(both, HALF // 2, 1))
    ahead = high_pair(sides, 0)
    for p in range(4):
        high, ahead = ahead, high_pair(sides, p + 1) if p < 3 else None
        sums = finish(0, p, own_lows[p], high, sums, store)
        if p < 3:
            lows_ref[p] = low_pair(low_sides, p)
    sums_ref[0] = sums[0]
    sums_ref[1] = sums[1]
    last_ref[0] = basis_ref[1, 7]
    for copy in copies:
        copy.wait()
    last_ref[1] = halo_basis[0]
    halo_ref[...] = halo_second[...]


def join_kernel(
    first_ref, sums_ref, lows_ref, last_ref, halo_ref, coarse_ref, log_ref, trace_ref,
    stage, log_stage, trace_stage, out_sem,
):
    early = [pltpu.make_async_copy(first_ref.at[p], coarse_ref.at[p, 0], out_sem.at[p]) for p in range(4)]
    late = [pltpu.make_async_copy(stage.at[p], coarse_ref.at[p, 1], out_sem.at[4 + p]) for p in range(4)]
    small = [
        pltpu.make_async_copy(log_stage, log_ref, out_sem.at[8]),
        pltpu.make_async_copy(trace_stage, trace_ref, out_sem.at[9]),
    ]
    for copy in early:
        copy.start()

    def store(p, value):
        stage[p] = value
        late[p].start()

    sides = high_sides([halo_ref[2 * p] for p in range(4)], [halo_ref[2 * p + 1] for p in range(4)])
    edge = spread([last_ref[0], last_ref[1]] + [last_ref[0]] * 6)
    last_sides = pair_sides(edge, pltpu.roll(edge, HALF - CHI, 1))
    sums = (sums_ref[0], sums_ref[1])
    ahead = lows_ref[0], high_pair(sides, 0)
    for p in range(4):
        low, high = ahead
        if p < 3:
            ahead = lows_ref[p + 1] if p < 2 else low_pair(last_sides, 0), high_pair(sides, p + 1)
        sums = finish(1, p, low, high, sums, store)
    squares, traces = sums
    norm = jnp.sqrt(squares)
    log_stage[...] = jnp.log(norm)[:2, :4]
    trace_stage[...] = (CHI * traces / norm)[:2, :4]
    for copy in small:
        copy.start()
    for copy in early + late + small:
        copy.wait()


def solution(mesh):
    nx, ny = mesh.shape["gx"], mesh.shape["gy"]
    vmem = pl.BlockSpec(memory_space=pltpu.VMEM)
    hbm = pl.BlockSpec(memory_space=pltpu.HBM)

    def body(site_tensors, test_matrix):
        site_tensors = pltpu.with_memory_space_constraint(site_tensors, pltpu.HBM)
        test_matrix = pltpu.with_memory_space_constraint(test_matrix, pltpu.HBM)
        between = pl.pallas_call(
            lambda *refs: split_kernel(nx, ny, *refs),
            out_shape=(
                pltpu.VMEM((4, WIDE, WIDE), BF16),
                pltpu.VMEM((2, 8, 128), F32),
                pltpu.VMEM((3, WIDE, WIDE), BF16),
                pltpu.VMEM((2, CHI, WIDE), BF16),
                pltpu.VMEM((8, CHI, WIDE), BF16),
            ),
            in_specs=[hbm, hbm],
            out_specs=(vmem,) * 5,
            scratch_shapes=[
                pltpu.VMEM((2, 8, WIDE, WIDE), BF16),
                pltpu.VMEM((2, 8, CHI, WIDE), BF16),
                pltpu.VMEM((8, CHI, WIDE), BF16),
                pltpu.VMEM((8, CHI, WIDE), BF16),
                pltpu.VMEM((1, CHI, WIDE), BF16),
                pltpu.VMEM((8, CHI, WIDE), BF16),
                pltpu.VMEM((8, 2, CHI, WIDE), BF16),
                pltpu.VMEM((4, WIDE, WIDE), BF16),
                pltpu.SemaphoreType.DMA((9,)),
                pltpu.SemaphoreType.DMA((3,)),
                pltpu.SemaphoreType.DMA((3,)),
            ],
            compiler_params=pltpu.CompilerParams(
                collective_id=0, has_side_effects=True, vmem_limit_bytes=24 * 2**20),
            cost_estimate=pl.CostEstimate(
                flops=700_000_000, bytes_accessed=3_000_000, transcendentals=0),
        )(site_tensors, test_matrix)
        between = [pltpu.with_memory_space_constraint(x, pltpu.VMEM) for x in between]
        coarse, log_norm, trace = pl.pallas_call(
            join_kernel,
            out_shape=(
                pltpu.HBM((4, 2, WIDE, WIDE), BF16),
                pltpu.HBM((2, 4), F32),
                pltpu.HBM((2, 4), F32),
            ),
            in_specs=[vmem] * 5,
            out_specs=(hbm, hbm, hbm),
            scratch_shapes=[
                pltpu.VMEM((4, WIDE, WIDE), BF16),
                pltpu.VMEM((2, 4), F32),
                pltpu.VMEM((2, 4), F32),
                pltpu.SemaphoreType.DMA((10,)),
            ],
            compiler_params=pltpu.CompilerParams(vmem_limit_bytes=24 * 2**20),
            cost_estimate=pl.CostEstimate(
                flops=300_000_000, bytes_accessed=1_000_000, transcendentals=0),
        )(*between)
        return coarse, log_norm.T, trace.T

    in_specs = (P("gx", "gy", None, None), P("gx", "gy", None, None))
    out_specs = (P("gx", "gy", None, None), P("gx", "gy"), P("gx", "gy"))
    return jax.shard_map(body, mesh=mesh, in_specs=in_specs, out_specs=out_specs, check_vma=False)
```

```python
import jax
import jax.numpy as jnp
from jax import lax
from jax.experimental import pallas as pl
from jax.experimental.pallas import tpu as pltpu
from jax.sharding import PartitionSpec as P

CHI = 16
WIDE = CHI * CHI
HALF = WIDE // 2
MESH = pl.DeviceIdType.MESH
F32 = jnp.float32
BF16 = jnp.bfloat16
NT = (((1,), (1,)), ((), ()))
NN = (((1,), (0,)), ((), ()))


def iota(shape, axis):
    return lax.broadcasted_iota(jnp.int32, shape, axis)


def swap_chunks(rows):
    rows = list(rows)
    chunk = iota(rows[0].shape, 1) // CHI
    for step in (4, 2, 1):
        low = (chunk & step) == 0
        for i in range(8):
            if i & step:
                continue
            first, other = rows[i], rows[i + step]
            if step == 4:
                moved = pltpu.roll(jnp.where(low, other, first), HALF // 2, 1)
                rows[i], rows[i + step] = jnp.where(low, first, moved), jnp.where(low, moved, other)
                continue
            rows[i] = jnp.where(low, first, pltpu.roll(other, CHI * step, 1))
            rows[i + step] = jnp.where(low, pltpu.roll(first, HALF - CHI * step, 1), other)
    return rows


def spread(halves):
    parts = []
    for side in range(2):
        parts += swap_chunks([h[:, side * HALF:(side + 1) * HALF] for h in halves])
    return jnp.concatenate(parts, axis=0)


def regroup(x):
    columns = []
    for upper in range(2):
        column = []
        for side in range(2):
            column += swap_chunks([
                x[(upper * 8 + v) * CHI:(upper * 8 + v + 1) * CHI, side * HALF:(side + 1) * HALF]
                for v in range(8)
            ])
        columns.append(jnp.concatenate(column, axis=0))
    return jnp.concatenate(columns, axis=1)


def eliminate(grams):
    row = iota(grams[0].shape, 0)
    lane = iota(grams[0].shape, 1)
    ids = range(len(grams))
    columns = [[jnp.take_along_axis(g, lane // CHI * CHI + k, axis=1) for k in range(CHI)] for g in grams]
    inverses = [jnp.where(row == lane % CHI, 1.0, 0.0).astype(F32)] * len(grams)
    pivots = list(grams)
    for k in range(CHI):
        pivot = [columns[s][k][k:k + 1] for s in ids]
        factor = [columns[s][k] * (1.0 / pivot[s]) for s in ids]
        for later in range(k + 1, CHI):
            for s in ids:
                columns[s][later] = columns[s][later] - factor[s] * columns[s][later][k:k + 1]
        for s in ids:
            pivots[s] = jnp.where(row == k, pivot[s], pivots[s])
            below = jnp.where(row > k, factor[s], 0.0)
            inverses[s] = inverses[s] - below * inverses[s][k:k + 1]
    return [i * lax.rsqrt(p) for i, p in zip(inverses, pivots)]


def flip_mask():
    row, col = iota((WIDE, WIDE), 0), iota((WIDE, WIDE), 1)
    return jnp.where((row // CHI == col % CHI) & (row % CHI == col // CHI), 1.0, 0.0).astype(F32)


def pair_sides(left, right):
    left = jnp.dot(flip_mask().astype(BF16), left, preferred_element_type=F32).astype(BF16)
    return left, right, left.T, right.T


def low_pair(sides, q):
    chunk = iota((WIDE, HALF), 1) // CHI
    masked = jnp.where(chunk == q, sides[1], jnp.zeros((), BF16))
    return regroup(jnp.dot(masked, sides[2], preferred_element_type=F32).astype(BF16))


def high_pair(sides, q):
    chunk = iota((WIDE, HALF), 1) // CHI
    masked = jnp.where(chunk == q, sides[0], jnp.zeros((), BF16))
    return regroup(jnp.dot(masked, sides[3], preferred_element_type=F32).astype(BF16))


def high_sides(south_east, south_west):
    turned = jnp.dot(
        jnp.concatenate(south_east, axis=0), flip_mask().astype(BF16), preferred_element_type=F32).astype(BF16)
    both = spread([turned[q * CHI:(q + 1) * CHI] for q in range(4)] + south_west)
    return pair_sides(both, pltpu.roll(both, HALF // 2, 1))


def finish(g, p, low, high, sums, store):
    squares, traces = sums
    raw = jnp.dot(low, high, preferred_element_type=F32)
    square = jnp.sum(jnp.sum(raw * raw, axis=0, keepdims=True), axis=1, keepdims=True) + 1e-6
    traced = jnp.sum(jnp.sum(raw * flip_mask(), axis=0, keepdims=True), axis=1, keepdims=True)
    store(p, (raw * (WIDE * lax.rsqrt(square))).astype(BF16))
    here = (iota((8, 128), 0) == g) & (iota((8, 128), 1) == p)
    return jnp.where(here, square, squares), jnp.where(here, traced, traces)


def split_kernel(
    nx, ny, tensors_ref, tests_ref, coarse_ref, sums_ref, lows_ref, last_ref, halo_ref,
    held, basis_ref, low_ref, up_ref, halo_basis, halo_second, tests, in_sem, send_sem, recv_sem,
):
    mx, my = lax.axis_index("gx"), lax.axis_index("gy")
    right, left = lax.rem(mx + 1, nx), lax.rem(mx + nx - 1, nx)
    above, below = lax.rem(my + 1, ny), lax.rem(my + ny - 1, ny)
    loads = [pltpu.make_async_copy(tensors_ref.at[c], held.at[c], in_sem.at[c]) for c in range(8)]
    loads.append(pltpu.make_async_copy(tests_ref, tests, in_sem.at[8]))
    loads[8].start()
    for load in loads[:8]:
        load.start()
    barrier = pltpu.get_barrier_semaphore()
    for target in ((right, my), (mx, above), (right, above)):
        pl.semaphore_signal(barrier, inc=1, device_id=target, device_id_type=MESH)

    loads[8].wait()
    chunk = iota((CHI, HALF), 1) // CHI
    parts, grams = [], []
    for side in range(2):
        sketches = []
        for n in range(8):
            x, y = 4 * side + n // 2, n % 2
            if y == 0:
                loads[x].wait()
            sketches.append(lax.dot_general(tests[x, y], held[x, y], NT, preferred_element_type=F32))
        part = jnp.concatenate(sketches, axis=0)
        product = lax.dot_general(part, part, NT, precision=lax.Precision.HIGHEST, preferred_element_type=F32)
        gram = product[:CHI]
        for n in range(1, 8):
            gram = jnp.where(chunk == n, product[n * CHI:(n + 1) * CHI], gram)
        parts.append(part)
        grams.append(gram)
    for side, inverse in enumerate(eliminate(grams)):
        block = jnp.concatenate([jnp.where(chunk == n, inverse, 0.0) for n in range(8)], axis=0)
        basis = jnp.dot(block, parts[side], precision=lax.Precision.HIGHEST, preferred_element_type=F32)
        basis_ref[pl.ds(8 * side, 8)] = basis.astype(BF16).reshape(8, CHI, WIDE)

    copies = [
        pltpu.make_async_remote_copy(
            basis_ref.at[1], halo_basis.at[0], send_sem.at[0], recv_sem.at[0],
            device_id=(left, my), device_id_type=MESH),
        pltpu.make_async_remote_copy(
            low_ref.at[0], halo_second.at[7], send_sem.at[1], recv_sem.at[1],
            device_id=(left, below), device_id_type=MESH),
        pltpu.make_async_remote_copy(
            low_ref.at[pl.ds(1, 7)], halo_second.at[pl.ds(0, 7)], send_sem.at[2], recv_sem.at[2],
            device_id=(mx, below), device_id_type=MESH),
    ]
    def send():
        pl.semaphore_wait(barrier, 3)
        for copy in copies:
            copy.start()

    for x in range(8):
        low_ref[x] = jnp.dot(basis_ref[2 * x], held[x, 0], preferred_element_type=F32).astype(BF16)
    first_chip = (my == 0) & (mx < 2)
    pl.when(jnp.logical_not(first_chip))(send)
    for x in range(8):
        up_ref[x] = jnp.dot(basis_ref[2 * x + 1], held[x, 1], preferred_element_type=F32).astype(BF16)

    def store(p, value):
        coarse_ref[p] = value

    sums = (jnp.ones((8, 128), F32), jnp.zeros((8, 128), F32))
    north_east = [basis_ref[4 * p] for p in range(4)] + [basis_ref[4 * p + 3] for p in range(4)]
    north_west = [basis_ref[4 * p + 2] for p in range(4)] + [basis_ref[4 * p + 5] for p in range(3)]
    low_sides = pair_sides(spread(north_east), spread(north_west + north_west[:1]))
    sides = high_sides([up_ref[2 * p] for p in range(4)], [up_ref[2 * p + 1] for p in range(4)])
    for p in range(3):
        lows_ref[p] = low_pair(low_sides, p + 4)
    ahead = low_pair(low_sides, 0), high_pair(sides, 0)
    pl.when(first_chip)(send)
    for p in range(4):
        (low, high), ahead = ahead, (low_pair(low_sides, p + 1), high_pair(sides, p + 1)) if p < 3 else None
        sums = finish(0, p, low, high, sums, store)
    sums_ref[0] = sums[0]
    sums_ref[1] = sums[1]
    last_ref[0] = basis_ref[15]
    for copy in copies:
        copy.wait()
    last_ref[1] = halo_basis[0]
    halo_ref[...] = halo_second[...]


def join_kernel(
    first_ref, sums_ref, lows_ref, last_ref, halo_ref, coarse_ref, log_ref, trace_ref,
    stage, log_stage, trace_stage, out_sem,
):
    early = [pltpu.make_async_copy(first_ref.at[p], coarse_ref.at[p, 0], out_sem.at[p]) for p in range(4)]
    late = [pltpu.make_async_copy(stage.at[p], coarse_ref.at[p, 1], out_sem.at[4 + p]) for p in range(4)]
    small = [
        pltpu.make_async_copy(log_stage, log_ref, out_sem.at[8]),
        pltpu.make_async_copy(trace_stage, trace_ref, out_sem.at[9]),
    ]
    for copy in early:
        copy.start()

    def store(p, value):
        stage[p] = value
        late[p].start()

    sides = high_sides([halo_ref[2 * p] for p in range(4)], [halo_ref[2 * p + 1] for p in range(4)])
    edge = spread([last_ref[0], last_ref[1]] + [last_ref[0]] * 6)
    last_sides = pair_sides(edge, pltpu.roll(edge, HALF - CHI, 1))
    sums = (sums_ref[0], sums_ref[1])
    ahead = lows_ref[0], high_pair(sides, 0)
    for p in range(4):
        low, high = ahead
        if p < 3:
            ahead = lows_ref[p + 1] if p < 2 else low_pair(last_sides, 0), high_pair(sides, p + 1)
        sums = finish(1, p, low, high, sums, store)
    squares, traces = sums
    norm = jnp.sqrt(squares)
    log_stage[...] = jnp.log(norm)[:2, :4]
    trace_stage[...] = (CHI * traces / norm)[:2, :4]
    for copy in small:
        copy.start()
    for copy in early + late + small:
        copy.wait()


def solution(mesh):
    nx, ny = mesh.shape["gx"], mesh.shape["gy"]
    vmem = pl.BlockSpec(memory_space=pltpu.VMEM)
    hbm = pl.BlockSpec(memory_space=pltpu.HBM)

    def body(site_tensors, test_matrix):
        site_tensors = pltpu.with_memory_space_constraint(site_tensors, pltpu.HBM)
        test_matrix = pltpu.with_memory_space_constraint(test_matrix, pltpu.HBM)
        between = pl.pallas_call(
            lambda *refs: split_kernel(nx, ny, *refs),
            out_shape=(
                pltpu.VMEM((4, WIDE, WIDE), BF16),
                pltpu.VMEM((2, 8, 128), F32),
                pltpu.VMEM((3, WIDE, WIDE), BF16),
                pltpu.VMEM((2, CHI, WIDE), BF16),
                pltpu.VMEM((8, CHI, WIDE), BF16),
            ),
            in_specs=[hbm, hbm],
            out_specs=(vmem,) * 5,
            scratch_shapes=[
                pltpu.VMEM((8, 2, WIDE, WIDE), BF16),
                pltpu.VMEM((16, CHI, WIDE), BF16),
                pltpu.VMEM((8, CHI, WIDE), BF16),
                pltpu.VMEM((8, CHI, WIDE), BF16),
                pltpu.VMEM((1, CHI, WIDE), BF16),
                pltpu.VMEM((8, CHI, WIDE), BF16),
                pltpu.VMEM((8, 2, CHI, WIDE), BF16),
                pltpu.SemaphoreType.DMA((9,)),
                pltpu.SemaphoreType.DMA((3,)),
                pltpu.SemaphoreType.DMA((3,)),
            ],
            compiler_params=pltpu.CompilerParams(
                collective_id=0, has_side_effects=True, vmem_limit_bytes=24 * 2**20),
            cost_estimate=pl.CostEstimate(
                flops=700_000_000, bytes_accessed=3_000_000, transcendentals=0),
        )(site_tensors, test_matrix)
        between = [pltpu.with_memory_space_constraint(x, pltpu.VMEM) for x in between]
        coarse, log_norm, trace = pl.pallas_call(
            join_kernel,
            out_shape=(
                pltpu.HBM((4, 2, WIDE, WIDE), BF16),
                pltpu.HBM((2, 4), F32),
                pltpu.HBM((2, 4), F32),
            ),
            in_specs=[vmem] * 5,
            out_specs=(hbm, hbm, hbm),
            scratch_shapes=[
                pltpu.VMEM((4, WIDE, WIDE), BF16),
                pltpu.VMEM((2, 4), F32),
                pltpu.VMEM((2, 4), F32),
                pltpu.SemaphoreType.DMA((10,)),
            ],
            compiler_params=pltpu.CompilerParams(vmem_limit_bytes=24 * 2**20),
            cost_estimate=pl.CostEstimate(
                flops=300_000_000, bytes_accessed=1_000_000, transcendentals=0),
        )(*between)
        return coarse, log_norm.T, trace.T

    in_specs = (P("gx", "gy", None, None), P("gx", "gy", None, None))
    out_specs = (P("gx", "gy", None, None), P("gx", "gy"), P("gx", "gy"))
    return jax.shard_map(body, mesh=mesh, in_specs=in_specs, out_specs=out_specs, check_vma=False)
```

```python
import jax
import jax.numpy as jnp
from jax import lax
from jax.experimental import pallas as pl
from jax.experimental.pallas import tpu as pltpu
from jax.sharding import PartitionSpec as P

CHI = 16
WIDE = CHI * CHI
HALF = WIDE // 2
MESH = pl.DeviceIdType.MESH
F32 = jnp.float32
BF16 = jnp.bfloat16
NT = (((1,), (1,)), ((), ()))
NN = (((1,), (0,)), ((), ()))


def iota(shape, axis):
    return lax.broadcasted_iota(jnp.int32, shape, axis)


def swap_chunks(rows):
    rows = list(rows)
    chunk = iota(rows[0].shape, 1) // CHI
    for step in (4, 2, 1):
        low = (chunk & step) == 0
        for i in range(8):
            if i & step:
                continue
            first, other = rows[i], rows[i + step]
            if step == 4:
                moved = pltpu.roll(jnp.where(low, other, first), HALF // 2, 1)
                rows[i], rows[i + step] = jnp.where(low, first, moved), jnp.where(low, moved, other)
                continue
            rows[i] = jnp.where(low, first, pltpu.roll(other, CHI * step, 1))
            rows[i + step] = jnp.where(low, pltpu.roll(first, HALF - CHI * step, 1), other)
    return rows


def spread(halves):
    parts = []
    for side in range(2):
        parts += swap_chunks([h[:, side * HALF:(side + 1) * HALF] for h in halves])
    return jnp.concatenate(parts, axis=0)


def regroup(x):
    columns = []
    for upper in range(2):
        column = []
        for side in range(2):
            column += swap_chunks([
                x[(upper * 8 + v) * CHI:(upper * 8 + v + 1) * CHI, side * HALF:(side + 1) * HALF]
                for v in range(8)
            ])
        columns.append(jnp.concatenate(column, axis=0))
    return jnp.concatenate(columns, axis=1)


def eliminate(grams):
    row = iota(grams[0].shape, 0)
    lane = iota(grams[0].shape, 1)
    ids = range(len(grams))
    columns = [[jnp.take_along_axis(g, lane // CHI * CHI + k, axis=1) for k in range(CHI)] for g in grams]
    inverses = [jnp.where(row == lane % CHI, 1.0, 0.0).astype(F32)] * len(grams)
    pivots = list(grams)
    for k in range(CHI):
        pivot = [columns[s][k][k:k + 1] for s in ids]
        factor = [columns[s][k] * (1.0 / pivot[s]) for s in ids]
        for later in range(k + 1, CHI):
            for s in ids:
                columns[s][later] = columns[s][later] - factor[s] * columns[s][later][k:k + 1]
        for s in ids:
            pivots[s] = jnp.where(row == k, pivot[s], pivots[s])
            below = jnp.where(row > k, factor[s], 0.0)
            inverses[s] = inverses[s] - below * inverses[s][k:k + 1]
    return [i * lax.rsqrt(p) for i, p in zip(inverses, pivots)]


def halves_of(x):
    high = x.astype(BF16)
    return high, (x - high.astype(F32)).astype(BF16)


def product_of(left, right, dims):
    rows = left[0].shape[0]
    main = lax.dot_general(jnp.concatenate(left, axis=0), right[0], dims, preferred_element_type=F32)
    return main[:rows] + (main[rows:] + lax.dot_general(left[0], right[1], dims, preferred_element_type=F32))


def flip_mask():
    row, col = iota((WIDE, WIDE), 0), iota((WIDE, WIDE), 1)
    return jnp.where((row // CHI == col % CHI) & (row % CHI == col // CHI), 1.0, 0.0).astype(F32)


def pair_sides(left, right):
    left = jnp.dot(flip_mask().astype(BF16), left, preferred_element_type=F32).astype(BF16)
    return left, right, left.T, right.T


def low_pair(sides, q):
    chunk = iota((WIDE, HALF), 1) // CHI
    masked = jnp.where(chunk == q, sides[1], jnp.zeros((), BF16))
    return regroup(jnp.dot(masked, sides[2], preferred_element_type=F32).astype(BF16))


def high_pair(sides, q):
    chunk = iota((WIDE, HALF), 1) // CHI
    masked = jnp.where(chunk == q, sides[0], jnp.zeros((), BF16))
    return regroup(jnp.dot(masked, sides[3], preferred_element_type=F32).astype(BF16))


def high_sides(south_east, south_west):
    turned = jnp.dot(
        jnp.concatenate(south_east, axis=0), flip_mask().astype(BF16), preferred_element_type=F32).astype(BF16)
    both = spread([turned[q * CHI:(q + 1) * CHI] for q in range(4)] + south_west)
    return pair_sides(both, pltpu.roll(both, HALF // 2, 1))


def finish(g, p, low, high, sums, store):
    squares, traces = sums
    raw = jnp.dot(low, high, preferred_element_type=F32)
    square = jnp.sum(jnp.sum(raw * raw, axis=0, keepdims=True), axis=1, keepdims=True) + 1e-6
    traced = jnp.sum(jnp.sum(raw * flip_mask(), axis=0, keepdims=True), axis=1, keepdims=True)
    store(p, (raw * (WIDE * lax.rsqrt(square))).astype(BF16))
    here = (iota((8, 128), 0) == g) & (iota((8, 128), 1) == p)
    return jnp.where(here, square, squares), jnp.where(here, traced, traces)


def split_kernel(
    nx, ny, tensors_ref, tests_ref, coarse_ref, sums_ref, lows_ref, last_ref, halo_ref,
    held, basis_ref, low_ref, up_ref, halo_basis, halo_second, tests, in_sem, send_sem, recv_sem,
):
    mx, my = lax.axis_index("gx"), lax.axis_index("gy")
    right, left = lax.rem(mx + 1, nx), lax.rem(mx + nx - 1, nx)
    above, below = lax.rem(my + 1, ny), lax.rem(my + ny - 1, ny)
    loads = [pltpu.make_async_copy(tensors_ref.at[c], held.at[c], in_sem.at[c]) for c in range(8)]
    loads.append(pltpu.make_async_copy(tests_ref, tests, in_sem.at[8]))
    loads[8].start()
    for load in loads[:8]:
        load.start()
    barrier = pltpu.get_barrier_semaphore()
    for target in ((right, my), (mx, above), (right, above)):
        pl.semaphore_signal(barrier, inc=1, device_id=target, device_id_type=MESH)

    loads[8].wait()
    chunk = iota((CHI, HALF), 1) // CHI
    parts, grams = [], []
    for side in range(2):
        sketches = []
        for n in range(8):
            x, y = 4 * side + n // 2, n % 2
            if y == 0:
                loads[x].wait()
            sketches.append(lax.dot_general(tests[x, y], held[x, y], NT, preferred_element_type=F32))
        part = halves_of(jnp.concatenate(sketches, axis=0))
        product = product_of(part, part, NT)
        gram = product[:CHI]
        for n in range(1, 8):
            gram = jnp.where(chunk == n, product[n * CHI:(n + 1) * CHI], gram)
        parts.append(part)
        grams.append(gram)
    for side, inverse in enumerate(eliminate(grams)):
        block = jnp.concatenate([jnp.where(chunk == n, inverse, 0.0) for n in range(8)], axis=0)
        basis = product_of(halves_of(block), parts[side], NN)
        basis_ref[pl.ds(8 * side, 8)] = basis.astype(BF16).reshape(8, CHI, WIDE)

    copies = [
        pltpu.make_async_remote_copy(
            basis_ref.at[1], halo_basis.at[0], send_sem.at[0], recv_sem.at[0],
            device_id=(left, my), device_id_type=MESH),
        pltpu.make_async_remote_copy(
            low_ref.at[0], halo_second.at[7], send_sem.at[1], recv_sem.at[1],
            device_id=(left, below), device_id_type=MESH),
        pltpu.make_async_remote_copy(
            low_ref.at[pl.ds(1, 3)], halo_second.at[pl.ds(0, 3)], send_sem.at[2], recv_sem.at[2],
            device_id=(mx, below), device_id_type=MESH),
        pltpu.make_async_remote_copy(
            low_ref.at[pl.ds(4, 4)], halo_second.at[pl.ds(3, 4)], send_sem.at[3], recv_sem.at[3],
            device_id=(mx, below), device_id_type=MESH),
    ]
    def send_early():
        pl.semaphore_wait(barrier, 3)
        for copy in copies[:3]:
            copy.start()

    def send_all():
        send_early()
        copies[3].start()

    first_chip = (my == 0) & (mx < 2)
    for x in range(4):
        low_ref[x] = jnp.dot(basis_ref[2 * x], held[x, 0], preferred_element_type=F32).astype(BF16)
    pl.when(jnp.logical_not(first_chip))(send_early)
    for x in range(4, 8):
        low_ref[x] = jnp.dot(basis_ref[2 * x], held[x, 0], preferred_element_type=F32).astype(BF16)
    pl.when(jnp.logical_not(first_chip))(copies[3].start)
    for x in range(8):
        up_ref[x] = jnp.dot(basis_ref[2 * x + 1], held[x, 1], preferred_element_type=F32).astype(BF16)

    def store(p, value):
        coarse_ref[p] = value

    sums = (jnp.ones((8, 128), F32), jnp.zeros((8, 128), F32))
    north_east = [basis_ref[4 * p] for p in range(4)] + [basis_ref[4 * p + 3] for p in range(4)]
    north_west = [basis_ref[4 * p + 2] for p in range(4)] + [basis_ref[4 * p + 5] for p in range(3)]
    low_sides = pair_sides(spread(north_east), spread(north_west + north_west[:1]))
    sides = high_sides([up_ref[2 * p] for p in range(4)], [up_ref[2 * p + 1] for p in range(4)])
    for p in range(3):
        lows_ref[p] = low_pair(low_sides, p + 4)
    ahead = low_pair(low_sides, 0), high_pair(sides, 0)
    pl.when(first_chip)(send_all)
    for p in range(4):
        (low, high), ahead = ahead, (low_pair(low_sides, p + 1), high_pair(sides, p + 1)) if p < 3 else None
        sums = finish(0, p, low, high, sums, store)
    sums_ref[0] = sums[0]
    sums_ref[1] = sums[1]
    last_ref[0] = basis_ref[15]
    for copy in copies:
        copy.wait()
    last_ref[1] = halo_basis[0]
    halo_ref[...] = halo_second[...]


def join_kernel(
    first_ref, sums_ref, lows_ref, last_ref, halo_ref, coarse_ref, log_ref, trace_ref,
    stage, log_stage, trace_stage, out_sem,
):
    early = [pltpu.make_async_copy(first_ref.at[p], coarse_ref.at[p, 0], out_sem.at[p]) for p in range(4)]
    late = [pltpu.make_async_copy(stage.at[p], coarse_ref.at[p, 1], out_sem.at[4 + p]) for p in range(4)]
    small = [
        pltpu.make_async_copy(log_stage, log_ref, out_sem.at[8]),
        pltpu.make_async_copy(trace_stage, trace_ref, out_sem.at[9]),
    ]
    for copy in early:
        copy.start()

    def store(p, value):
        stage[p] = value
        late[p].start()

    sides = high_sides([halo_ref[2 * p] for p in range(4)], [halo_ref[2 * p + 1] for p in range(4)])
    edge = spread([last_ref[0], last_ref[1]] + [last_ref[0]] * 6)
    last_sides = pair_sides(edge, pltpu.roll(edge, HALF - CHI, 1))
    sums = (sums_ref[0], sums_ref[1])
    ahead = lows_ref[0], high_pair(sides, 0)
    for p in range(4):
        low, high = ahead
        if p < 3:
            ahead = lows_ref[p + 1] if p < 2 else low_pair(last_sides, 0), high_pair(sides, p + 1)
        sums = finish(1, p, low, high, sums, store)
    squares, traces = sums
    norm = jnp.sqrt(squares)
    log_stage[...] = jnp.log(norm)[:2, :4]
    trace_stage[...] = (CHI * traces / norm)[:2, :4]
    for copy in small:
        copy.start()
    for copy in early + late + small:
        copy.wait()


def solution(mesh):
    nx, ny = mesh.shape["gx"], mesh.shape["gy"]
    vmem = pl.BlockSpec(memory_space=pltpu.VMEM)
    hbm = pl.BlockSpec(memory_space=pltpu.HBM)

    def body(site_tensors, test_matrix):
        site_tensors = pltpu.with_memory_space_constraint(site_tensors, pltpu.HBM)
        test_matrix = pltpu.with_memory_space_constraint(test_matrix, pltpu.HBM)
        between = pl.pallas_call(
            lambda *refs: split_kernel(nx, ny, *refs),
            out_shape=(
                pltpu.VMEM((4, WIDE, WIDE), BF16),
                pltpu.VMEM((2, 8, 128), F32),
                pltpu.VMEM((3, WIDE, WIDE), BF16),
                pltpu.VMEM((2, CHI, WIDE), BF16),
                pltpu.VMEM((8, CHI, WIDE), BF16),
            ),
            in_specs=[hbm, hbm],
            out_specs=(vmem,) * 5,
            scratch_shapes=[
                pltpu.VMEM((8, 2, WIDE, WIDE), BF16),
                pltpu.VMEM((16, CHI, WIDE), BF16),
                pltpu.VMEM((8, CHI, WIDE), BF16),
                pltpu.VMEM((8, CHI, WIDE), BF16),
                pltpu.VMEM((1, CHI, WIDE), BF16),
                pltpu.VMEM((8, CHI, WIDE), BF16),
                pltpu.VMEM((8, 2, CHI, WIDE), BF16),
                pltpu.SemaphoreType.DMA((9,)),
                pltpu.SemaphoreType.DMA((4,)),
                pltpu.SemaphoreType.DMA((4,)),
            ],
            compiler_params=pltpu.CompilerParams(
                collective_id=0, has_side_effects=True, vmem_limit_bytes=24 * 2**20),
            cost_estimate=pl.CostEstimate(
                flops=700_000_000, bytes_accessed=3_000_000, transcendentals=0),
        )(site_tensors, test_matrix)
        between = [pltpu.with_memory_space_constraint(x, pltpu.VMEM) for x in between]
        coarse, log_norm, trace = pl.pallas_call(
            join_kernel,
            out_shape=(
                pltpu.HBM((4, 2, WIDE, WIDE), BF16),
                pltpu.HBM((2, 4), F32),
                pltpu.HBM((2, 4), F32),
            ),
            in_specs=[vmem] * 5,
            out_specs=(hbm, hbm, hbm),
            scratch_shapes=[
                pltpu.VMEM((4, WIDE, WIDE), BF16),
                pltpu.VMEM((2, 4), F32),
                pltpu.VMEM((2, 4), F32),
                pltpu.SemaphoreType.DMA((10,)),
            ],
            compiler_params=pltpu.CompilerParams(vmem_limit_bytes=24 * 2**20),
            cost_estimate=pl.CostEstimate(
                flops=300_000_000, bytes_accessed=1_000_000, transcendentals=0),
        )(*between)
        return coarse, log_norm.T, trace.T

    in_specs = (P("gx", "gy", None, None), P("gx", "gy", None, None))
    out_specs = (P("gx", "gy", None, None), P("gx", "gy"), P("gx", "gy"))
    return jax.shard_map(body, mesh=mesh, in_specs=in_specs, out_specs=out_specs, check_vma=False)
```
